128 devices in a mesh: gx: 16 (over x, y_hi, core), gy: 8 (over z, y_lo).
Axes of the slice: x: 4, y: 4 (y_hi: 2, y_lo: 2; y = y_hi * 2 + y_lo), z: 4, core: 2. Of those that a mesh axis runs over, the one named last changes fastest.
Arguments:
- features: bfloat16 [96, 32, 64, 128], P(None, 'gx', 'gy'), may hold values from -6 to 6
- cotangent: bfloat16 [96, 32, 64, 128], P(None, 'gx', 'gy'), may hold values from -6 to 6
- weights: bfloat16 [27, 96, 96], replicated, may hold values from -0.125 to 0.125
- ground: int32 [32, 64], P('gx', 'gy'), may hold values from 0 to 31
- thick: int32 [32, 64], P('gx', 'gy'), may hold values from 48 to 96
Outputs:
- outputs: bfloat16 [96, 32, 64, 128], P(None, 'gx', 'gy')
- input_grad: bfloat16 [96, 32, 64, 128], P(None, 'gx', 'gy')
- weight_grad: float32 [27, 96, 96], replicated
The draws below stay inside these ranges and needn't reach their ends.
All inputs are finite; a program needn't handle non-finite values.
Results may differ from the reference program's by a relative error of at most 0.001.
Values may be sent and summed in bfloat16 or wider, within the bound.
A program may use at most 128 MiB of HBM per device.

```python
import math
import jax
import jax.numpy as jnp
from jax import lax

C = 96
OFFSETS = 27
NZ = 128
NX = 32
NY = 64


def plant(result, key, smallest, top_value):
    place = [jax.random.randint(jax.random.fold_in(key, axis), (), 0, length) for axis, length in enumerate(result.shape)]
    main_axis = result.shape.index(max(result.shape))
    beside = place[:main_axis] + [(place[main_axis] + 1) % result.shape[main_axis]] + place[main_axis + 1:]
    return result.at[tuple(place)].set(smallest).at[tuple(beside)].set(top_value)


def block_scale(own_key, shape, shards, least, top_value):
    level = 1.0
    for dim, shards_of in shards:
        steps = jax.random.uniform(jax.random.fold_in(jax.random.fold_in(own_key, 6), dim), (shards_of,), jnp.float32, least / len(shards), top_value / len(shards))
        level = level * jnp.repeat(jnp.exp(steps), shape[dim] // shards_of).reshape((-1,) + (1,) * (len(shape) - 1 - dim))
    return level


def bell_draw(key, shape, width, most, split=(), kind=jnp.bfloat16):
    result = width * jax.random.normal(key, shape, jnp.float32)
    if split:
        result = result * block_scale(key, shape, split, -0.22, 0.18)
    return jnp.clip(result, -most, most).astype(kind)


def setup_inputs(seed: int = 0) -> dict:
    streams_of = jax.random.split(jax.random.key(seed), 6)
    return {
        "features": bell_draw(streams_of[0], (C, NX, NY, NZ), 1.0, 6.0, ((1, 16), (2, 8))),
        "cotangent": bell_draw(streams_of[1], (C, NX, NY, NZ), 1.0, 6.0, ((1, 16), (2, 8))),
        "weights": bell_draw(streams_of[2], (OFFSETS, C, C), (OFFSETS * C) ** -0.5, 0.125),
        "ground": plant(jax.random.randint(streams_of[3], (NX, NY), 0, NZ // 4), jax.random.fold_in(streams_of[3], 1), 0, (NZ // 4) - 1).astype(jnp.int32),
        "thick": plant(jax.random.randint(streams_of[4], (NX, NY), 3 * NZ // 8, 3 * NZ // 4 + 1), jax.random.fold_in(streams_of[4], 1), 3 * NZ // 8, (3 * NZ // 4 + 1) - 1).astype(jnp.int32),
    }


def occupancy(ground, thick, depth_z):
    heights = jnp.arange(depth_z, dtype=jnp.int32)
    lower = heights[None, None, :] >= ground[:, :, None]
    upper = heights[None, None, :] < (ground + thick)[:, :, None]
    return (lower & upper).astype(jnp.bfloat16)

def reference(features, cotangent, weights, ground, thick):
    occupied = occupancy(ground, thick, NZ)
    masked_in = features * occupied[None]
    masked_cot = cotangent * occupied[None]
    widths = ((0, 0), (1, 1), (1, 1), (1, 1))
    padded_in = jnp.pad(masked_in, widths)
    padded_cot = jnp.pad(masked_cot, widths)
    cot_flat = masked_cot.reshape(C, -1)
    forward_sum = jnp.zeros((C, NX * NY * NZ), jnp.float32)
    backward_sum = jnp.zeros((C, NX * NY * NZ), jnp.float32)
    grad_list = []
    for offset in range(27):
        step_x = offset // 9 - 1
        step_y = offset // 3 % 3 - 1
        step_z = offset % 3 - 1
        moved_in = padded_in[:, 1 + step_x:1 + step_x + NX, 1 + step_y:1 + step_y + NY, 1 + step_z:1 + step_z + NZ].reshape(C, -1)
        moved_cot = padded_cot[:, 1 - step_x:1 - step_x + NX, 1 - step_y:1 - step_y + NY, 1 - step_z:1 - step_z + NZ].reshape(C, -1)
        forward_sum = forward_sum + jnp.dot(weights[offset], moved_in, preferred_element_type=jnp.float32)
        backward_sum = backward_sum + jnp.dot(weights[offset].T, moved_cot, preferred_element_type=jnp.float32)
        grad_list.append(lax.dot_general(cot_flat, moved_in, (((1,), (1,)), ((), ())), preferred_element_type=jnp.float32))
    occupied_flat = occupied.reshape(1, -1)
    outputs = (forward_sum * occupied_flat).astype(jnp.bfloat16).reshape(C, NX, NY, NZ)
    input_grad = (backward_sum * occupied_flat).astype(jnp.bfloat16).reshape(C, NX, NY, NZ)
    grad_scale = 1.0 / math.sqrt(NX * NY * NZ)
    weight_grad = jnp.stack(grad_list, 0) * grad_scale
    return (outputs, input_grad, weight_grad)
```

```python
import math

import jax
import jax.numpy as jnp
from jax import lax
from jax.experimental import pallas as pl
from jax.experimental.pallas import tpu as pltpu
from jax.sharding import PartitionSpec as P

MESH = pl.DeviceIdType.MESH
F32 = jnp.float32
BF16 = jnp.bfloat16
C = 96
NX, NY, NZ = 2, 8, 128
TILES = 256
HALF = 128
NEAR, FAR, SAME = 0, 1, 2
NT = (((1,), (1,)), ((), ()))


def kernel(
    scale,
    feat, cot, w, ground, thick,
    out, grad_in, grad_w,
    pf, pc, tmp, shifted, lf, lb, acc, red, r0, r1, r2, r3, full, tout,
    halo_send, halo_recv, rs_send, rs_recv, ag_send, ag_recv, core_send, core_recv,
):
    gx = lax.axis_index("gx")
    gy = lax.axis_index("gy")
    core = lax.rem(gx, 2)
    y_hi = lax.rem(lax.div(gx, 2), 2)
    cx = lax.div(gx, 4)
    y_lo = lax.rem(gy, 2)
    cz = lax.div(gy, 2)
    cy = y_hi * 2 + y_lo
    near_gx = gx + 1 - 2 * core
    far_gx = gx - 1 + 2 * core
    has_far = jnp.logical_and(far_gx >= 0, far_gx < 16)
    x_first = 1 - core

    def chip(x, y, z):
        return (x * 4 + lax.div(y, 2) * 2 + core, z * 2 + lax.rem(y, 2))

    def peer(stage, d):
        first = 1 - core if stage == 1 else core
        if stage == 3:
            return chip(cx, lax.rem(cy + d, 4), cz)
        return chip(lax.rem(cx + d * first, 4), cy, lax.rem(cz + d * (1 - first), 4))

    pos = {
        1: cx * (1 - core) + cz * core,
        2: cz * (1 - core) + cx * core,
        3: cy,
    }

    has_dy = {-1: gy > 0, 0: None, 1: gy < 7}

    def present(side, dy):
        terms = []
        if side == FAR:
            terms.append(has_far)
        if dy != 0:
            terms.append(has_dy[dy])
        if not terms:
            return None
        return terms[0] if len(terms) == 1 else jnp.logical_and(*terms)

    def when(cond, fn):
        if cond is None:
            fn()
        else:
            pl.when(cond)(fn)

    def halo_device(side, dy):
        return ({NEAR: near_gx, FAR: far_gx, SAME: gx}[side], gy + dy)

    halos = [(s, dy) for s in (FAR, NEAR, SAME) for dy in (0, -1, 1) if (s, dy) != (SAME, 0)]

    barrier = pltpu.get_barrier_semaphore()
    for side, dy in halos:
        def greet(side=side, dy=dy):
            pl.semaphore_signal(barrier, inc=1, device_id=halo_device(side, dy), device_id_type=MESH)
        when(present(side, dy), greet)
    pl.semaphore_signal(barrier, inc=1, device_id=(near_gx, gy), device_id_type=MESH)
    for stage in (1, 2, 3):
        for d in (1, 2, 3):
            pl.semaphore_signal(barrier, inc=1, device_id=peer(stage, d), device_id_type=MESH)

    rows = lax.broadcasted_iota(jnp.int32, (NY, NZ), 0)
    heights = lax.broadcasted_iota(jnp.int32, (NY, NZ), 1)

    def occupied(x):
        low = jnp.zeros((NY, NZ), jnp.int32)
        high = jnp.zeros((NY, NZ), jnp.int32)
        for y in range(NY):
            g = ground[x, y]
            low = jnp.where(rows == y, g, low)
            high = jnp.where(rows == y, g + thick[x, y], high)
        return jnp.logical_and(heights >= low, heights < high)

    occ = [occupied(x) for x in range(NX)]

    def columns(src, dst, x, shifts):
        value = jnp.where(occ[x][None], src[:, x].astype(F32), 0.0)
        tmp[...] = value.reshape(C * NY, NZ)
        for y in range(NY):
            col = tmp[pl.ds(y, C, stride=NY), :]
            dst[x + 1, y + 1] = col.astype(BF16)
            if shifts:
                lanes = slice(y * NZ, (y + 1) * NZ)
                shifted[x, 0:C, lanes] = pltpu.roll(col, NZ - 1, 1).astype(BF16)
                shifted[x, C : 2 * C, lanes] = col.astype(BF16)
                shifted[x, 2 * C : 3 * C, lanes] = pltpu.roll(col, 1, 1).astype(BF16)

    for x in range(NX):
        columns(feat, pf, x, False)

    n_dy = jnp.where(gy > 0, 1, 0) + jnp.where(gy < 7, 1, 0)
    n_far = jnp.where(has_far, 1, 0)
    pl.semaphore_wait(barrier, (n_dy + 1) * (2 + n_far) - 1 + 10)

    src_y = {-1: 1, 0: 1, 1: NY}
    dst_y = {-1: NY + 1, 0: 1, 1: 0}
    len_y = {-1: 1, 0: NY, 1: 1}

    def halo_copy(which, side, dy):
        buf = (pf, pc)[which]
        n = len_y[dy]
        if side == SAME:
            src_x = dst_x = pl.ds(1, 2)
        elif side == NEAR:
            src_x, dst_x = pl.ds(2 - core, 1), pl.ds(3 * core, 1)
        else:
            src_x, dst_x = pl.ds(1 + core, 1), pl.ds(3 * (1 - core), 1)
        return pltpu.make_async_remote_copy(
            src_ref=buf.at[src_x, pl.ds(src_y[dy], n)],
            dst_ref=buf.at[dst_x, pl.ds(dst_y[dy], n)],
            send_sem=halo_send.at[which, side, dy + 1],
            recv_sem=halo_recv.at[which, side, dy + 1],
            device_id=halo_device(side, dy),
            device_id_type=MESH,
        )

    def send_halos(which):
        for side, dy in halos:
            when(present(side, dy), lambda side=side, dy=dy: halo_copy(which, side, dy).start())

    def recv_halos(which, sides):
        for side, dy in halos:
            if side in sides:
                when(present(side, -dy), lambda side=side, dy=dy: halo_copy(which, side, dy).wait_recv())

    def done_halos(which):
        for side, dy in halos:
            when(present(side, dy), lambda side=side, dy=dy: halo_copy(which, side, dy).wait_send())

    def clear_edges(buf):
        zeros = jnp.zeros((C, NZ), BF16)

        def far_side():
            for y in range(NY + 2):
                buf[3 * core, y] = zeros

        def y_side(y):
            for x in range(NX + 2):
                buf[x, y] = zeros

        pl.when(jnp.logical_not(has_far))(far_side)
        pl.when(gy == 0)(lambda: y_side(0))
        pl.when(gy == 7)(lambda: y_side(NY + 1))

    send_halos(0)
    for x in range(NX):
        columns(cot, pc, x, True)
    clear_edges(pf)
    clear_edges(pc)

    for c in range(3):
        lf[c * C : (c + 1) * C, :] = jnp.concatenate([w[ab * 3 + c] for ab in range(9)], axis=1)
        lb[c * C : (c + 1) * C, :] = jnp.concatenate(
            [w[26 - (ab * 3 + c)].T for ab in range(9)], axis=1
        )

    def weight_terms(x):
        stack = jnp.concatenate(
            [
                jnp.concatenate([pf[x + a, y + b] for y in range(NY)], axis=1)
                for a in range(3)
                for b in range(3)
            ],
            axis=0,
        )
        return lax.dot_general(shifted[x], stack, NT, preferred_element_type=F32)

    recv_halos(0, (NEAR, SAME))
    acc[...] = weight_terms(x_first)
    recv_halos(0, (FAR,))
    send_halos(1)
    total = acc[...] + weight_terms(1 - x_first)
    for i in range(36):
        for j in range(7):
            tile = total[i * 8 : (i + 1) * 8, j * 128 : min((j + 1) * 128, 9 * C)]
            if j == 6:
                tile = jnp.concatenate([tile, jnp.zeros((8, 32), F32)], axis=1)
            red[i * 7 + j] = tile
    red[252:256] = jnp.zeros((4, 8, 128), F32)

    def conv_pair(x, j, buf, lhs):
        stack = jnp.concatenate(
            [
                jnp.concatenate([buf[x + a, 2 * j + b], buf[x + a, 2 * j + b + 1]], axis=1)
                for a in range(3)
                for b in range(3)
            ],
            axis=0,
        )
        prod = jnp.dot(lhs[...], stack, preferred_element_type=F32)
        for half in range(2):
            part = prod[:, half * NZ : (half + 1) * NZ]
            col = (
                pltpu.roll(part[0:C], 1, 1) + part[C : 2 * C] + pltpu.roll(part[2 * C : 3 * C], NZ - 1, 1)
            )
            tout[pl.ds(2 * j + half, C, stride=NY), :] = col

    def conv(x, buf, lhs, dst):
        for j in range(NY // 2):
            conv_pair(x, j, buf, lhs)
        mask = occupied(x)
        dst[:, x] = jnp.where(mask[None], tout[...].reshape(C, NY, NZ), 0.0).astype(BF16)

    core_device = (near_gx, gy)

    def core_copy(k, src, dst):
        return pltpu.make_async_remote_copy(
            src_ref=src, dst_ref=dst, send_sem=core_send.at[k], recv_sem=core_recv.at[k],
            device_id=core_device, device_id_type=MESH,
        )

    mine = core * HALF
    first = core_copy(0, red.at[pl.ds((1 - core) * HALF, HALF)], r0)
    first.start()
    recv_halos(1, (NEAR, SAME))
    conv(x_first, pf, lf, out)
    first.wait_recv()
    red[pl.ds(mine, HALF)] = red[pl.ds(mine, HALF)] + r0[...]

    size = HALF
    base = mine
    boxes = {1: r1, 2: r2, 3: r3}
    bases = {}
    sent = [first]
    work = {
        1: lambda: conv(1 - x_first, pf, lf, out),
        2: lambda: conv(x_first, pc, lb, grad_in),
        3: lambda: (recv_halos(1, (FAR,)), conv(1 - x_first, pc, lb, grad_in)),
    }
    for stage in (1, 2, 3):
        size //= 4
        copies = []
        for d in (1, 2, 3):
            target = lax.rem(pos[stage] + d, 4)
            copies.append(
                pltpu.make_async_remote_copy(
                    src_ref=red.at[pl.ds(base + target * size, size)],
                    dst_ref=boxes[stage].at[d - 1],
                    send_sem=rs_send.at[stage - 1, d - 1],
                    recv_sem=rs_recv.at[stage - 1, d - 1],
                    device_id=peer(stage, d),
                    device_id_type=MESH,
                )
            )
        for copy in copies:
            copy.start()
        sent += copies
        work[stage]()
        base = base + pos[stage] * size
        bases[stage] = base
        total = red[pl.ds(base, size)]
        for d in (1, 2, 3):
            copies[d - 1].wait_recv()
            total = total + boxes[stage][d - 1]
        if stage < 3:
            red[pl.ds(base, size)] = total
        else:
            full[pl.ds(base, size)] = total * scale

    for stage in (3, 2, 1):
        here = full.at[pl.ds(bases[stage], size)]
        copies = [
            pltpu.make_async_remote_copy(
                src_ref=here, dst_ref=here,
                send_sem=ag_send.at[stage - 1, d - 1],
                recv_sem=ag_recv.at[stage - 1, d - 1],
                device_id=peer(stage, d),
                device_id_type=MESH,
            )
            for d in (1, 2, 3)
        ]
        for copy in copies:
            copy.start()
        for copy in copies:
            copy.wait_recv()
        sent += copies
        size *= 4
    mine_full = full.at[pl.ds(mine, HALF)]
    last = core_copy(1, mine_full, mine_full)
    last.start()
    sent.append(last)
    done_halos(0)
    done_halos(1)
    last.wait_recv()

    for i in range(36):
        row = jnp.concatenate([full[i * 7 + j] for j in range(7)], axis=1)
        c, o = i // 12, (i % 12) * 8
        for ab in range(9):
            grad_w[ab * 3 + c, o : o + 8, :] = row[:, ab * C : (ab + 1) * C]
    for copy in sent:
        copy.wait_send()


def shards(features, cotangent, weights, ground, thick):
    voxels = NX * NY * NZ * lax.axis_size("gx") * lax.axis_size("gy")
    block = jax.ShapeDtypeStruct((C, NX, NY, NZ), BF16)
    vmem = pl.BlockSpec(memory_space=pltpu.VMEM)
    smem = pl.BlockSpec(memory_space=pltpu.SMEM)

    def body(*refs):
        kernel(1.0 / math.sqrt(voxels), *refs)

    return pl.pallas_call(
        body,
        out_shape=(block, block, jax.ShapeDtypeStruct((27, C, C), F32)),
        in_specs=[vmem, vmem, vmem, smem, smem],
        out_specs=(vmem, vmem, vmem),
        scratch_shapes=[
            pltpu.VMEM((NX + 2, NY + 2, C, NZ), BF16),
            pltpu.VMEM((NX + 2, NY + 2, C, NZ), BF16),
            pltpu.VMEM((C * NY, NZ), F32),
            pltpu.VMEM((NX, 3 * C, NY * NZ), BF16),
            pltpu.VMEM((3 * C, 9 * C), BF16),
            pltpu.VMEM((3 * C, 9 * C), BF16),
            pltpu.VMEM((3 * C, 9 * C), F32),
            pltpu.VMEM((TILES, 8, 128), F32),
            pltpu.VMEM((HALF, 8, 128), F32),
            pltpu.VMEM((3, HALF // 4, 8, 128), F32),
            pltpu.VMEM((3, HALF // 16, 8, 128), F32),
            pltpu.VMEM((3, HALF // 64, 8, 128), F32),
            pltpu.VMEM((TILES, 8, 128), F32),
            pltpu.VMEM((C * NY, NZ), F32),
            pltpu.SemaphoreType.DMA((2, 3, 3)),
            pltpu.SemaphoreType.DMA((2, 3, 3)),
            pltpu.SemaphoreType.DMA((3, 3)),
            pltpu.SemaphoreType.DMA((3, 3)),
            pltpu.SemaphoreType.DMA((3, 3)),
            pltpu.SemaphoreType.DMA((3, 3)),
            pltpu.SemaphoreType.DMA((2,)),
            pltpu.SemaphoreType.DMA((2,)),
        ],
        compiler_params=pltpu.CompilerParams(
            collective_id=0, has_side_effects=True, vmem_limit_bytes=56 * 1024 * 1024
        ),
        cost_estimate=pl.CostEstimate(
            flops=3 * 2 * NX * NY * NZ * 27 * C * C, bytes_accessed=4 * 2**20, transcendentals=0
        ),
    )(features, cotangent, weights, ground, thick)


def solution(mesh):
    assert mesh.shape["gx"] == 16 and mesh.shape["gy"] == 8
    placed = (
        P(None, "gx", "gy", None),
        P(None, "gx", "gy", None),
        P(),
        P("gx", "gy"),
        P("gx", "gy"),
    )
    return jax.shard_map(
        shards,
        mesh=mesh,
        in_specs=placed,
        out_specs=(P(None, "gx", "gy", None), P(None, "gx", "gy", None), P()),
        check_vma=False,
    )
```

```python
import math

import jax
import jax.numpy as jnp
from jax import lax
from jax.experimental import pallas as pl
from jax.experimental.pallas import tpu as pltpu
from jax.sharding import PartitionSpec as P

MESH = pl.DeviceIdType.MESH
F32 = jnp.float32
BF16 = jnp.bfloat16
C = 96
NX, NY, NZ = 2, 8, 128
OWNERS = 54
LANES = 128
NEAR, FAR, SAME = 0, 1, 2
NT = (((1,), (1,)), ((), ()))


def kernel(
    scale,
    feat_hbm, cot_hbm, w_hbm, ground, thick,
    out_hbm, grad_in_hbm, grad_w_hbm,
    feat, cot, w, out, grad_in, pf, pc, tmp, shifted, lf, lb, red, core_box, late_box, mid_box, full, tout,
    load_sem, store_sem, halo_send, halo_recv, core_send, core_recv,
    rs_send, rs_recv, ag_send, ag_recv, plane_sem, cube_sem,
):
    gx = lax.axis_index("gx")
    gy = lax.axis_index("gy")
    core = lax.rem(gx, 2)
    cx = lax.div(gx, 4)
    cy = lax.rem(lax.div(gx, 2), 2) * 2 + lax.rem(gy, 2)
    cz = lax.div(gy, 2)
    near_gx = gx + 1 - 2 * core
    far_gx = gx - 1 + 2 * core
    has_far = jnp.logical_and(far_gx >= 0, far_gx < 16)
    near_x = 1 - core
    far_x = core
    near_a = 2 * (1 - core)
    far_a = 2 * core

    loads = [
        pltpu.make_async_copy(feat_hbm, feat, load_sem.at[0]),
        pltpu.make_async_copy(cot_hbm, cot, load_sem.at[1]),
        pltpu.make_async_copy(w_hbm, w, load_sem.at[2]),
    ]
    for load in loads:
        load.start()

    def chip(x, y, z):
        return (x * 4 + lax.div(y, 2) * 2 + core, z * 2 + lax.rem(y, 2))

    def step(dx, dy, dz):
        return lax.rem(cx + dx, 4), lax.rem(cy + dy, 4), lax.rem(cz + dz, 4)

    has_dy = {-1: gy > 0, 0: None, 1: gy < 7}

    def present(side, dy):
        terms = []
        if side == FAR:
            terms.append(has_far)
        if dy != 0:
            terms.append(has_dy[dy])
        if not terms:
            return None
        return terms[0] if len(terms) == 1 else jnp.logical_and(*terms)

    def when(cond, fn):
        if cond is None:
            fn()
        else:
            pl.when(cond)(fn)

    def halo_device(side, dy):
        return ({NEAR: near_gx, FAR: far_gx, SAME: gx}[side], gy + dy)

    halos = [(s, dy) for s in (FAR, SAME, NEAR) for dy in (0, -1, 1) if (s, dy) != (SAME, 0)]
    rings = {
        "x": [chip(*step(d, 0, 0)) for d in (1, 2, 3)],
        "y": [chip(*step(0, d, 0)) for d in (1, 2, 3)],
        "z": [chip(*step(0, 0, d)) for d in (1, 2, 3)],
    }

    def signal(sem, device):
        pl.semaphore_signal(sem, inc=1, device_id=device, device_id_type=MESH)

    barrier = pltpu.get_barrier_semaphore()
    for side, dy in halos:
        when(present(side, dy), lambda side=side, dy=dy: signal(barrier, halo_device(side, dy)))
    for axis in "xyz":
        for device in rings[axis]:
            signal(barrier, device)

    rows = lax.broadcasted_iota(jnp.int32, (NY, NZ), 0)
    heights = lax.broadcasted_iota(jnp.int32, (NY, NZ), 1)

    def occupied(x):
        low = jnp.zeros((NY, NZ), jnp.int32)
        high = jnp.zeros((NY, NZ), jnp.int32)
        for y in range(NY):
            g = ground[x, y]
            low = jnp.where(rows == y, g, low)
            high = jnp.where(rows == y, g + thick[x, y], high)
        return jnp.logical_and(heights >= low, heights < high)

    def columns(src, dst, x, shifts):
        value = jnp.where(occupied(x)[None], src[:, x].astype(F32), 0.0)
        tmp[...] = value.reshape(C * NY, NZ)
        for y in range(NY):
            col = tmp[pl.ds(y, C, stride=NY), :]
            dst[x + 1, y + 1] = col.astype(BF16)
            if shifts:
                lanes = slice(y * NZ, (y + 1) * NZ)
                shifted[x, 0:C, lanes] = pltpu.roll(col, NZ - 1, 1).astype(BF16)
                shifted[x, C : 2 * C, lanes] = col.astype(BF16)
                shifted[x, 2 * C : 3 * C, lanes] = pltpu.roll(col, 1, 1).astype(BF16)

    loads[0].wait()
    for x in range(NX):
        columns(feat, pf, x, False)

    n_dy = jnp.where(gy > 0, 1, 0) + jnp.where(gy < 7, 1, 0)
    n_far = jnp.where(has_far, 1, 0)
    pl.semaphore_wait(barrier, (n_dy + 1) * (2 + n_far) - 1 + 9)

    src_y = {-1: 1, 0: 1, 1: NY}
    dst_y = {-1: NY + 1, 0: 1, 1: 0}
    len_y = {-1: 1, 0: NY, 1: 1}

    def halo_copy(which, side, dy):
        buf = (pf, pc)[which]
        n = len_y[dy]
        if side == SAME:
            src_x = dst_x = pl.ds(1, 2)
        elif side == NEAR:
            src_x, dst_x = pl.ds(2 - core, 1), pl.ds(3 * core, 1)
        else:
            src_x, dst_x = pl.ds(1 + core, 1), pl.ds(3 * (1 - core), 1)
        return pltpu.make_async_remote_copy(
            src_ref=buf.at[src_x, pl.ds(src_y[dy], n)],
            dst_ref=buf.at[dst_x, pl.ds(dst_y[dy], n)],
            send_sem=halo_send.at[which, side, dy + 1],
            recv_sem=halo_recv.at[which, side, dy + 1],
            device_id=halo_device(side, dy),
            device_id_type=MESH,
        )

    def send_halos(which):
        for side, dy in halos:
            when(present(side, dy), lambda side=side, dy=dy: halo_copy(which, side, dy).start())

    def recv_halos(which, sides):
        for side, dy in halos:
            if side in sides:
                when(present(side, -dy), lambda side=side, dy=dy: halo_copy(which, side, dy).wait_recv())

    def done_halos(which, sides):
        for side, dy in halos:
            if side in sides:
                when(present(side, dy), lambda side=side, dy=dy: halo_copy(which, side, dy).wait_send())

    def clear_edges(buf):
        zeros = jnp.zeros((C, NZ), BF16)

        def far_side():
            for y in range(NY + 2):
                buf[3 * core, y] = zeros

        def y_side(y):
            for x in range(NX + 2):
                buf[x, y] = zeros

        pl.when(jnp.logical_not(has_far))(far_side)
        pl.when(gy == 0)(lambda: y_side(0))
        pl.when(gy == 7)(lambda: y_side(NY + 1))

    send_halos(0)
    for device in rings["z"]:
        signal(plane_sem, device)
    loads[1].wait()
    for x in range(NX):
        columns(cot, pc, x, True)
    send_halos(1)
    clear_edges(pf)
    clear_edges(pc)
    pl.semaphore_wait(plane_sem, 3)
    for device in rings["y"]:
        signal(cube_sem, device)

    loads[2].wait()
    for c in range(3):
        lf[c * C : (c + 1) * C, :] = jnp.concatenate([w[ab * 3 + c] for ab in range(9)], axis=1)
        lb[c * C : (c + 1) * C, :] = jnp.concatenate(
            [w[26 - (ab * 3 + c)].T for ab in range(9)], axis=1
        )

    def weight_terms(xs, a, b):
        lhs = jnp.concatenate([shifted[x] for x in xs], axis=1)
        rhs = jnp.concatenate([pf[x + a, y + b] for x in xs for y in range(NY)], axis=1)
        return lax.dot_general(lhs, rhs, NT, preferred_element_type=F32)

    def put(a, b, value, add):
        for c in range(3):
            k = a * 9 + b * 3 + c
            part = value[c * C : (c + 1) * C]
            red[k, :, 0:C] = red[k, :, 0:C] + part if add else part

    recv_halos(0, (NEAR, SAME))
    for b in range(3):
        put(near_a, b, weight_terms((near_x, far_x), near_a, b), False)
    for b in range(3):
        put(1, b, weight_terms((near_x, far_x), 1, b), False)

    def core_copy(k, src, dst):
        return pltpu.make_async_remote_copy(
            src_ref=src, dst_ref=dst, send_sem=core_send.at[k], recv_sem=core_recv.at[k],
            device_id=(near_gx, gy), device_id_type=MESH,
        )

    other = 1 - core

    def core_parts(m):
        return [
            (pl.ds(18 * m, 9), slice(None), pl.ds(0, 9)),
            (pl.ds(9 + 5 * m, 4), slice(None), pl.ds(9, 4)),
            (pl.ds(13, 1), pl.ds(48 * m, 48), pl.ds(13, 1)),
        ]

    pairs = []
    for i, (ks, rs, box) in enumerate(core_parts(other)):
        dst = core_box.at[box] if i < 2 else core_box.at[box, pl.ds(0, 48)]
        src = red.at[ks] if i < 2 else red.at[ks, rs]
        pairs.append(core_copy(i, src, dst))
    for pair in pairs:
        pair.start()
    for b in range(3):
        put(far_a, b, weight_terms((near_x,), far_a, b), False)

    def conv_pair(x, j, buf, lhs):
        stack = jnp.concatenate(
            [
                jnp.concatenate([buf[x + a, 2 * j + b], buf[x + a, 2 * j + b + 1]], axis=1)
                for a in range(3)
                for b in range(3)
            ],
            axis=0,
        )
        prod = jnp.dot(lhs[...], stack, preferred_element_type=F32)
        for half in range(2):
            part = prod[:, half * NZ : (half + 1) * NZ]
            col = (
                pltpu.roll(part[0:C], 1, 1) + part[C : 2 * C] + pltpu.roll(part[2 * C : 3 * C], NZ - 1, 1)
            )
            tout[pl.ds(2 * j + half, C, stride=NY), :] = col

    def conv(x, buf, lhs, dst):
        for j in range(NY // 2):
            conv_pair(x, j, buf, lhs)
        mask = occupied(x)
        dst[:, x] = jnp.where(mask[None], tout[...].reshape(C, NY, NZ), 0.0).astype(BF16)

    me = cx * 16 + cy * 4 + cz

    def late_share(buf, j):
        return buf.at[far_a * 9 + lax.div(j, 6), pl.ds(pl.multiple_of(lax.rem(j, 6) * 16, 16), 16)]

    def mid_share(buf, j):
        t = 54 * core + j
        return buf.at[9 + lax.div(t, 12), pl.ds(pl.multiple_of(lax.rem(t, 12) * 8, 8), 8)]

    others = sorted(
        [(dx, dy, dz) for dx in range(4) for dy in range(4) for dz in range(4) if (dx, dy, dz) != (0, 0, 0)],
        key=lambda d: -sum(min(v, 4 - v) for v in d),
    )

    def exchange(index, share, box):
        for dx, dy, dz in others:
            x, y, z = step(dx, dy, dz)
            j = x * 16 + y * 4 + z

            @pl.when(j < OWNERS)
            def _(x=x, y=y, z=z, j=j, d=dx * 16 + dy * 4 + dz):
                pltpu.make_async_remote_copy(
                    src_ref=share(red, j), dst_ref=box.at[d],
                    send_sem=rs_send.at[index], recv_sem=rs_recv.at[index],
                    device_id=chip(x, y, z), device_id_type=MESH,
                ).start()

    def drain(ref, sem):
        pltpu.make_async_copy(ref, ref, sem).wait()

    def collect(index, share, box):
        @pl.when(me < OWNERS)
        def _():
            drain(box.at[pl.ds(1, 63)], rs_recv.at[index])
            total = share(red, me)[...] + jnp.sum(box[1:64], axis=0)
            share(full, me)[...] = total * scale
            for dx, dy, dz in others:
                x, y, z = step(dx, dy, dz)
                pltpu.make_async_remote_copy(
                    src_ref=share(full, me), dst_ref=share(full, me),
                    send_sem=ag_send.at[index], recv_sem=ag_recv.at[index],
                    device_id=chip(x, y, z), device_id_type=MESH,
                ).start()

    def shares_wait(sem, box, n):
        drain(box.at[pl.ds(0, n)], sem)

    def gathered(sem, box):
        pl.when(me < OWNERS)(lambda: shares_wait(sem, box, OWNERS - 1))
        pl.when(me >= OWNERS)(lambda: shares_wait(sem, box, OWNERS))

    conv(near_x, pf, lf, out)
    for pair in pairs:
        pair.wait_recv()
    for i, (ks, rs, box) in enumerate(core_parts(core)):
        if i < 2:
            red[ks] = red[ks] + core_box[box]
        else:
            red[ks, rs] = red[ks, rs] + core_box[box, 0:48]
    pl.semaphore_wait(cube_sem, 3)
    exchange(0, mid_share, mid_box)
    recv_halos(0, (FAR,))
    for b in range(3):
        put(far_a, b, weight_terms((far_x,), far_a, b), True)
    exchange(1, late_share, late_box)
    conv(far_x, pf, lf, out)
    stores = [pltpu.make_async_copy(out, out_hbm, store_sem.at[0])]
    stores[0].start()
    recv_halos(1, (NEAR, SAME))
    conv(near_x, pc, lb, grad_in)
    collect(0, mid_share, mid_box)
    collect(1, late_share, late_box)
    recv_halos(1, (FAR,))
    conv(far_x, pc, lb, grad_in)
    stores.append(pltpu.make_async_copy(grad_in, grad_in_hbm, store_sem.at[1]))
    stores[1].start()

    gathered(ag_recv.at[0], mid_box)
    gathered(ag_recv.at[1], late_box)
    finals = []
    for i, (ks, rs, _) in enumerate(core_parts(core)):
        ref = full.at[ks] if i < 2 else full.at[ks, rs]
        finals.append(core_copy(3 + i, ref, ref))
    for copy in finals:
        copy.start()
    done_halos(0, (NEAR, SAME, FAR))
    done_halos(1, (NEAR, SAME, FAR))
    for copy in pairs:
        copy.wait_send()
    for index, box in enumerate((mid_box, late_box)):
        gathered(rs_send.at[index], box)
        pl.when(me < OWNERS)(lambda index=index, box=box: shares_wait(ag_send.at[index], box, 63))
    for copy in finals:
        copy.wait_recv()
    stores.append(pltpu.make_async_copy(full, grad_w_hbm, store_sem.at[2]))
    stores[2].start()
    for copy in finals:
        copy.wait_send()
    for store in stores:
        store.wait()


def hand_on(a, b, c, x, y, z, va, vb, vc, vz, load_sem, store_sem):
    loads = [
        pltpu.make_async_copy(src, dst, load_sem.at[i]) for i, (src, dst) in enumerate(((c, vc), (a, va), (b, vb)))
    ]
    stores = [
        pltpu.make_async_copy(src, dst, store_sem.at[i]) for i, (src, dst) in enumerate(((vz, z), (va, x), (vb, y)))
    ]
    for load in loads:
        load.start()
    loads[0].wait()
    vz[...] = vc[:, :, 0:C]
    for i in range(3):
        if i:
            loads[i].wait()
        stores[i].start()
    for store in stores:
        store.wait()


def shards(features, cotangent, weights, ground, thick):
    voxels = NX * NY * NZ * lax.axis_size("gx") * lax.axis_size("gy")
    block = jax.ShapeDtypeStruct((C, NX, NY, NZ), BF16)
    shapes = (block, block, jax.ShapeDtypeStruct((27, C, C), F32))
    hbm = pl.BlockSpec(memory_space=pl.ANY)
    smem = pl.BlockSpec(memory_space=pltpu.SMEM)

    def body(*refs):
        kernel(1.0 / math.sqrt(voxels), *refs)

    dma = pltpu.SemaphoreType.DMA
    results = pl.pallas_call(
        body,
        out_shape=(block, block, jax.ShapeDtypeStruct((27, C, LANES), F32)),
        in_specs=[hbm, hbm, hbm, smem, smem],
        out_specs=(hbm, hbm, hbm),
        scratch_shapes=[
            pltpu.VMEM((C, NX, NY, NZ), BF16),
            pltpu.VMEM((C, NX, NY, NZ), BF16),
            pltpu.VMEM((27, C, C), BF16),
            pltpu.VMEM((C, NX, NY, NZ), BF16),
            pltpu.VMEM((C, NX, NY, NZ), BF16),
            pltpu.VMEM((NX + 2, NY + 2, C, NZ), BF16),
            pltpu.VMEM((NX + 2, NY + 2, C, NZ), BF16),
            pltpu.VMEM((C * NY, NZ), F32),
            pltpu.VMEM((NX, 3 * C, NY * NZ), BF16),
            pltpu.VMEM((3 * C, 9 * C), BF16),
            pltpu.VMEM((3 * C, 9 * C), BF16),
            pltpu.VMEM((27, C, LANES), F32),
            pltpu.VMEM((14, C, LANES), F32),
            pltpu.VMEM((64, 16, LANES), F32),
            pltpu.VMEM((64, 8, LANES), F32),
            pltpu.VMEM((27, C, LANES), F32),
            pltpu.VMEM((C * NY, NZ), F32),
            dma((3,)),
            dma((3,)),
            dma((2, 3, 3)),
            dma((2, 3, 3)),
            dma((6,)),
            dma((6,)),
            dma((2,)),
            dma((2,)),
            dma((2,)),
            dma((2,)),
            pltpu.SemaphoreType.REGULAR,
            pltpu.SemaphoreType.REGULAR,
        ],
        compiler_params=pltpu.CompilerParams(
            collective_id=0, has_side_effects=True, vmem_limit_bytes=56 * 1024 * 1024
        ),
        cost_estimate=pl.CostEstimate(
            flops=3 * 2 * NX * NY * NZ * 27 * C * C, bytes_accessed=4 * 2**20, transcendentals=0
        ),
    )(features, cotangent, weights, ground, thick)
    return pl.pallas_call(
        hand_on,
        out_shape=shapes,
        in_specs=[hbm] * 3,
        out_specs=(hbm,) * 3,
        scratch_shapes=[
            pltpu.VMEM((C, NX, NY, NZ), BF16),
            pltpu.VMEM((C, NX, NY, NZ), BF16),
            pltpu.VMEM((27, C, LANES), F32),
            pltpu.VMEM((27, C, C), F32),
            dma((3,)),
            dma((3,)),
        ],
        compiler_params=pltpu.CompilerParams(vmem_limit_bytes=60 * 1024 * 1024),
    )(*results)


def solution(mesh):
    assert mesh.shape["gx"] == 16 and mesh.shape["gy"] == 8
    placed = (
        P(None, "gx", "gy", None),
        P(None, "gx", "gy", None),
        P(),
        P("gx", "gy"),
        P("gx", "gy"),
    )
    return jax.shard_map(
        shards,
        mesh=mesh,
        in_specs=placed,
        out_specs=(P(None, "gx", "gy", None), P(None, "gx", "gy", None), P()),
        check_vma=False,
    )
```

```python
import math

import jax
import jax.numpy as jnp
from jax import lax
from jax.experimental import pallas as pl
from jax.experimental.pallas import tpu as pltpu
from jax.sharding import PartitionSpec as P

MESH = pl.DeviceIdType.MESH
F32 = jnp.float32
BF16 = jnp.bfloat16
C = 96
NX, NY, NZ = 2, 8, 128
OWNERS = 14
BLOCK = 84
NEAR, FAR, SAME = 0, 1, 2
NT = (((1,), (1,)), ((), ()))


def kernel(
    scale,
    feat_hbm, cot_hbm, w_hbm, ground, thick,
    out, grad_in, full,
    feat, cot, w, pf, pc, tmp, shifted, lf, lb, red, core_box, late_box, mid_box, late_ring, mid_ring, tout,
    load_sem, halo_send, halo_recv, core_send, core_recv,
    rs_send, rs_recv, ag_send, ag_recv, ring_send, ring_recv, plane_sem,
):
    gx = lax.axis_index("gx")
    gy = lax.axis_index("gy")
    core = lax.rem(gx, 2)
    cx = lax.div(gx, 4)
    cy = lax.rem(lax.div(gx, 2), 2) * 2 + lax.rem(gy, 2)
    cz = lax.div(gy, 2)
    near_gx = gx + 1 - 2 * core
    far_gx = gx - 1 + 2 * core
    has_far = jnp.logical_and(far_gx >= 0, far_gx < 16)
    near_x = 1 - core
    far_x = core
    near_a = 2 * (1 - core)
    far_a = 2 * core

    loads = [
        pltpu.make_async_copy(feat_hbm, feat, load_sem.at[0]),
        pltpu.make_async_copy(cot_hbm, cot, load_sem.at[1]),
        pltpu.make_async_copy(w_hbm, w, load_sem.at[2]),
    ]
    for load in loads:
        load.start()

    def chip(x, y, z):
        return (x * 4 + lax.div(y, 2) * 2 + core, z * 2 + lax.rem(y, 2))

    def step(dx, dy, dz):
        return lax.rem(cx + dx, 4), lax.rem(cy + dy, 4), lax.rem(cz + dz, 4)

    has_dy = {-1: gy > 0, 0: None, 1: gy < 7}

    def present(side, dy):
        terms = []
        if side == FAR:
            terms.append(has_far)
        if dy != 0:
            terms.append(has_dy[dy])
        if not terms:
            return None
        return terms[0] if len(terms) == 1 else jnp.logical_and(*terms)

    def when(cond, fn):
        if cond is None:
            fn()
        else:
            pl.when(cond)(fn)

    def halo_device(side, dy):
        return ({NEAR: near_gx, FAR: far_gx, SAME: gx}[side], gy + dy)

    halos = [(SAME, -1), (SAME, 1), (FAR, 0), (FAR, -1), (FAR, 1), (NEAR, 0)]
    rings = {
        "x": [chip(*step(d, 0, 0)) for d in (1, 2, 3)],
        "y": [chip(*step(0, d, 0)) for d in (1, 2, 3)],
        "z": [chip(*step(0, 0, d)) for d in (1, 2, 3)],
    }

    def signal(sem, device):
        pl.semaphore_signal(sem, inc=1, device_id=device, device_id_type=MESH)

    barrier = pltpu.get_barrier_semaphore()
    for side, dy in halos:
        when(present(side, dy), lambda side=side, dy=dy: signal(barrier, halo_device(side, dy)))
    for axis in "xyz":
        for device in rings[axis]:
            signal(barrier, device)

    rows = lax.broadcasted_iota(jnp.int32, (NY, NZ), 0)
    heights = lax.broadcasted_iota(jnp.int32, (NY, NZ), 1)

    def occupied(x):
        low = jnp.zeros((NY, NZ), jnp.int32)
        high = jnp.zeros((NY, NZ), jnp.int32)
        for y in range(NY):
            g = ground[x, y]
            low = jnp.where(rows == y, g, low)
            high = jnp.where(rows == y, g + thick[x, y], high)
        return jnp.logical_and(heights >= low, heights < high)

    def columns(src, dst, x, shifts):
        value = jnp.where(occupied(x)[None], src[:, x].astype(F32), 0.0)
        tmp[...] = value.reshape(C * NY, NZ)
        for y in range(NY):
            col = tmp[pl.ds(y, C, stride=NY), :]
            dst[x + 1, y + 1] = col.astype(BF16)
            if shifts:
                lanes = slice(y * NZ, (y + 1) * NZ)
                shifted[x, 0:C, lanes] = pltpu.roll(col, NZ - 1, 1).astype(BF16)
                shifted[x, C : 2 * C, lanes] = col.astype(BF16)
                shifted[x, 2 * C : 3 * C, lanes] = pltpu.roll(col, 1, 1).astype(BF16)

    loads[0].wait()
    for x in range(NX):
        columns(feat, pf, x, False)

    n_dy = jnp.where(gy > 0, 1, 0) + jnp.where(gy < 7, 1, 0)
    n_far = jnp.where(has_far, 1, 0)
    pl.semaphore_wait(barrier, n_dy + n_far * (n_dy + 1) + 1 + 9)

    src_y = {-1: 1, 0: 1, 1: NY}
    dst_y = {-1: NY + 1, 0: 1, 1: 0}
    len_y = {-1: 1, 0: NY, 1: 1}

    def halo_copy(which, side, dy):
        buf = (pf, pc)[which]
        n = len_y[dy]
        if side == SAME:
            src_x = dst_x = pl.ds(1, 2)
        elif side == NEAR:
            src_x, dst_x = pl.ds(2 - core, 1), pl.ds(3 * core, 1)
        else:
            src_x, dst_x = pl.ds(1 + core, 1), pl.ds(3 * (1 - core), 1)
        return pltpu.make_async_remote_copy(
            src_ref=buf.at[src_x, pl.ds(src_y[dy], n)],
            dst_ref=buf.at[dst_x, pl.ds(dst_y[dy], n)],
            send_sem=halo_send.at[which, side, dy + 1],
            recv_sem=halo_recv.at[which, side, dy + 1],
            device_id=halo_device(side, dy),
            device_id_type=MESH,
        )

    def send_halos(which):
        for side, dy in halos:
            when(present(side, dy), lambda side=side, dy=dy: halo_copy(which, side, dy).start())

    def recv_halos(which, sides):
        for side, dy in halos:
            if side in sides:
                when(present(side, -dy), lambda side=side, dy=dy: halo_copy(which, side, dy).wait_recv())

    def done_halos(which, sides):
        for side, dy in halos:
            if side in sides:
                when(present(side, dy), lambda side=side, dy=dy: halo_copy(which, side, dy).wait_send())

    def corner_copy(which, e):
        buf = (pf, pc)[which]
        y = pl.ds(0 if e < 0 else NY + 1, 1)
        return pltpu.make_async_remote_copy(
            src_ref=buf.at[pl.ds(2 - core, 1), y],
            dst_ref=buf.at[pl.ds(3 * core, 1), y],
            send_sem=halo_send.at[which, NEAR, e + 1],
            recv_sem=halo_recv.at[which, NEAR, e + 1],
            device_id=(near_gx, gy),
            device_id_type=MESH,
        )

    def corners(which, act):
        for e in (-1, 1):
            pl.when(has_dy[e])(lambda e=e: act(corner_copy(which, e)))

    def clear_edges(buf):
        zeros = jnp.zeros((C, NZ), BF16)

        def far_side():
            for y in range(NY + 2):
                buf[3 * core, y] = zeros

        def y_side(y):
            for x in range(NX + 2):
                buf[x, y] = zeros

        pl.when(jnp.logical_not(has_far))(far_side)
        pl.when(gy == 0)(lambda: y_side(0))
        pl.when(gy == 7)(lambda: y_side(NY + 1))

    send_halos(0)
    for device in rings["z"]:
        signal(plane_sem, device)
    loads[1].wait()
    for x in range(NX):
        columns(cot, pc, x, True)
    clear_edges(pf)
    clear_edges(pc)

    loads[2].wait()
    for c in range(3):
        lf[c * C : (c + 1) * C, :] = jnp.concatenate([w[ab * 3 + c] for ab in range(9)], axis=1)
        lb[c * C : (c + 1) * C, :] = jnp.concatenate(
            [w[26 - (ab * 3 + c)].T for ab in range(9)], axis=1
        )

    def weight_terms(xs, a):
        lhs = jnp.concatenate([shifted[x] for x in xs], axis=1)
        rhs = jnp.concatenate(
            [
                jnp.concatenate([pf[x + a, y + b] for x in xs for y in range(NY)], axis=1)
                for b in range(3)
            ],
            axis=0,
        )
        return lax.dot_general(lhs, rhs, NT, preferred_element_type=F32)

    def put(a, value, add):
        rest = jnp.concatenate([value[72 * q : 72 * q + 72, 256:288] for q in range(4)], axis=1)
        parts = (
            (0, 36, value[:, 0:128]), (36, 36, value[:, 128:256]), (72, 9, rest),
        )
        for start, n, part in parts:
            at = pl.ds(BLOCK * a + start, n)
            part = part.reshape(n, 8, 128)
            red[at] = red[at] + part if add else part
        if not add:
            red[pl.ds(BLOCK * a + 81, 3)] = jnp.zeros((3, 8, 128), F32)

    def core_copy(k, src, dst):
        return pltpu.make_async_remote_copy(
            src_ref=src, dst_ref=dst, send_sem=core_send.at[k], recv_sem=core_recv.at[k],
            device_id=(near_gx, gy), device_id_type=MESH,
        )

    def late_part(buf, m):
        return buf.at[pl.ds(2 * BLOCK * m, BLOCK)]

    def mid_part(buf, m):
        return buf.at[pl.ds(BLOCK + BLOCK // 2 * m, BLOCK // 2)]

    other = 1 - core
    recv_halos(0, (SAME,))
    corners(0, lambda copy: copy.start())
    put(1, weight_terms((near_x, far_x), 1), False)
    pairs = [core_copy(0, mid_part(red, other), core_box.at[pl.ds(BLOCK, BLOCK // 2)])]
    pairs[0].start()
    recv_halos(0, (NEAR,))
    corners(0, lambda copy: copy.wait_recv())
    put(near_a, weight_terms((near_x, far_x), near_a), False)
    pairs.append(core_copy(1, late_part(red, other), core_box.at[pl.ds(0, BLOCK)]))
    pairs[1].start()
    put(far_a, weight_terms((near_x,), far_a), False)

    def conv_pair(x, j, buf, lhs):
        stack = jnp.concatenate(
            [
                jnp.concatenate([buf[x + a, 2 * j + b], buf[x + a, 2 * j + b + 1]], axis=1)
                for a in range(3)
                for b in range(3)
            ],
            axis=0,
        )
        prod = jnp.dot(lhs[...], stack, preferred_element_type=F32)
        for half in range(2):
            part = prod[:, half * NZ : (half + 1) * NZ]
            col = (
                pltpu.roll(part[0:C], 1, 1) + part[C : 2 * C] + pltpu.roll(part[2 * C : 3 * C], NZ - 1, 1)
            )
            tout[pl.ds(2 * j + half, C, stride=NY), :] = col

    def conv(x, buf, lhs, dst):
        for j in range(NY // 2):
            conv_pair(x, j, buf, lhs)
        mask = occupied(x)
        dst[:, x] = jnp.where(mask[None], tout[...].reshape(C, NY, NZ), 0.0).astype(BF16)

    me = cx * 4 + cz
    plane = sorted(
        [(dx, dz) for dx in range(4) for dz in range(4) if (dx, dz) != (0, 0)],
        key=lambda d: -sum(min(v, 4 - v) for v in d),
    )

    def late_share(buf, j):
        return buf.at[pl.ds(2 * BLOCK * core + 6 * j, 6)]

    def mid_share(buf, j):
        return buf.at[pl.ds(BLOCK + BLOCK // 2 * core + 3 * j, 3)]

    shares = (mid_share, late_share)
    boxes = (mid_box, late_box)
    circles = (mid_ring, late_ring)

    def exchange(index):
        for dx, dz in plane:
            x, y, z = step(dx, 0, dz)
            j = x * 4 + z

            @pl.when(j < OWNERS)
            def _(device=chip(x, y, z), j=j, d=dx * 4 + dz):
                pltpu.make_async_remote_copy(
                    src_ref=shares[index](red, j), dst_ref=boxes[index].at[d],
                    send_sem=rs_send.at[index], recv_sem=rs_recv.at[index],
                    device_id=device, device_id_type=MESH,
                ).start()

    def drain(ref, sem):
        pltpu.make_async_copy(ref, ref, sem).wait()

    def owner(fn):
        pl.when(me < OWNERS)(fn)

    def collect(index):
        @owner
        def _():
            drain(boxes[index].at[pl.ds(1, 15)], rs_recv.at[index])
            circles[index][cy] = shares[index](red, me)[...] + jnp.sum(boxes[index][1:16], axis=0)
            for device in rings["y"]:
                here = circles[index].at[cy]
                pltpu.make_async_remote_copy(
                    src_ref=here, dst_ref=here, send_sem=ring_send.at[index], recv_sem=ring_recv.at[index],
                    device_id=device, device_id_type=MESH,
                ).start()

    def hand_out(index, j, device, d):
        share = shares[index](full, j)
        return pltpu.make_async_remote_copy(
            src_ref=share, dst_ref=share, send_sem=ag_send.at[index], recv_sem=ag_recv.at[index, d],
            device_id=device, device_id_type=MESH,
        )

    def pass_on(index, j):
        share = shares[index](full, j)
        core_copy(2 + index, share, share).start()

    def finish(index):
        @owner
        def _():
            drain(circles[index].at[pl.ds(0, 3)], ring_recv.at[index])
            terms = [circles[index][y] for y in range(4)]
            shares[index](full, me)[...] = ((terms[0] + terms[1]) + (terms[2] + terms[3])) * scale
            for dx, dz in plane:
                hand_out(index, me, chip(*step(dx, 0, dz)), dx * 4 + dz).start()
            pass_on(index, me)

    def gather(index):
        for dx, dz in reversed(plane):
            x, y, z = step(4 - dx, 0, 4 - dz)
            j = x * 4 + z

            @pl.when(j < OWNERS)
            def _(device=chip(x, y, z), j=j, d=dx * 4 + dz):
                hand_out(index, j, device, d).wait_recv()
                pass_on(index, j)

    pl.semaphore_wait(plane_sem, 3)
    for pair in pairs:
        pair.wait_recv()
    mid = mid_part(red, core)
    mid[...] = mid[...] + core_box[BLOCK : BLOCK + BLOCK // 2]
    exchange(0)
    late = late_part(red, core)
    late[...] = late[...] + core_box[0:BLOCK]
    recv_halos(0, (FAR,))
    put(far_a, weight_terms((far_x,), far_a), True)
    exchange(1)
    send_halos(1)
    conv(near_x, pf, lf, out)
    conv(far_x, pf, lf, out)
    collect(0)
    recv_halos(1, (SAME, NEAR))
    corners(1, lambda copy: copy.start())
    corners(1, lambda copy: copy.wait_recv())
    collect(1)
    conv(near_x, pc, lb, grad_in)
    finish(0)
    finish(1)
    gather(0)
    recv_halos(1, (FAR,))
    conv(far_x, pc, lb, grad_in)
    gather(1)
    for which in range(2):
        done_halos(which, (NEAR, SAME, FAR))
        corners(which, lambda copy: copy.wait_send())
    for copy in pairs:
        copy.wait_send()
    for index, box in enumerate(boxes):
        owner(lambda: drain(box.at[pl.ds(0, OWNERS - 1)], rs_send.at[index]))
        pl.when(me >= OWNERS)(lambda: drain(box.at[pl.ds(0, OWNERS)], rs_send.at[index]))
        owner(lambda: drain(circles[index].at[pl.ds(0, 3)], ring_send.at[index]))
        owner(lambda: drain(box.at[pl.ds(0, 15)], ag_send.at[index]))
    for index, part in enumerate((mid_part, late_part)):
        passed = part(full, other)
        core_copy(2 + index, passed, passed).wait()


def hand_on(a, b, c, x, y, z):
    x[...] = a[...]
    y[...] = b[...]
    for k in range(3):
        tiles = c[BLOCK * k : BLOCK * k + 81]
        left = tiles[0:36].reshape(3 * C, 128)
        right = tiles[36:72].reshape(3 * C, 128)
        rest = tiles[72:81].reshape(72, 128)
        rest = jnp.concatenate([rest[:, 32 * q : 32 * q + 32] for q in range(4)], axis=0)
        blocks = (
            left[:, 0:C],
            jnp.concatenate([left[:, C:128], right[:, 0:64]], axis=1),
            jnp.concatenate([right[:, 64:128], rest], axis=1),
        )
        for i, block in enumerate(blocks):
            z[9 * k + 3 * i : 9 * k + 3 * i + 3] = block.reshape(3, C, C)


def shards(features, cotangent, weights, ground, thick):
    voxels = NX * NY * NZ * lax.axis_size("gx") * lax.axis_size("gy")
    block = jax.ShapeDtypeStruct((C, NX, NY, NZ), BF16)
    hbm = pl.BlockSpec(memory_space=pltpu.HBM)
    vmem = pl.BlockSpec(memory_space=pltpu.VMEM)
    smem = pl.BlockSpec(memory_space=pltpu.SMEM)

    def body(*refs):
        kernel(1.0 / math.sqrt(voxels), *refs)

    dma = pltpu.SemaphoreType.DMA
    inner = pltpu.VMEM((C, NX, NY, NZ), BF16)
    results = pl.pallas_call(
        body,
        out_shape=(inner, inner, pltpu.VMEM((3 * BLOCK, 8, 128), F32)),
        in_specs=[hbm, hbm, hbm, smem, smem],
        out_specs=(vmem, vmem, vmem),
        scratch_shapes=[
            inner,
            inner,
            pltpu.VMEM((27, C, C), BF16),
            pltpu.VMEM((NX + 2, NY + 2, C, NZ), BF16),
            pltpu.VMEM((NX + 2, NY + 2, C, NZ), BF16),
            pltpu.VMEM((C * NY, NZ), F32),
            pltpu.VMEM((NX, 3 * C, NY * NZ), BF16),
            pltpu.VMEM((3 * C, 9 * C), BF16),
            pltpu.VMEM((3 * C, 9 * C), BF16),
            pltpu.VMEM((3 * BLOCK, 8, 128), F32),
            pltpu.VMEM((BLOCK + BLOCK // 2, 8, 128), F32),
            pltpu.VMEM((16, 6, 8, 128), F32),
            pltpu.VMEM((16, 3, 8, 128), F32),
            pltpu.VMEM((4, 6, 8, 128), F32),
            pltpu.VMEM((4, 3, 8, 128), F32),
            pltpu.VMEM((C * NY, NZ), F32),
            dma((3,)),
            dma((2, 3, 3)),
            dma((2, 3, 3)),
            dma((4,)),
            dma((4,)),
            dma((2,)),
            dma((2,)),
            dma((2,)),
            dma((2, 16)),
            dma((2,)),
            dma((2,)),
            pltpu.SemaphoreType.REGULAR,
        ],
        compiler_params=pltpu.CompilerParams(
            collective_id=0, has_side_effects=True, vmem_limit_bytes=48 * 1024 * 1024
        ),
        cost_estimate=pl.CostEstimate(
            flops=3 * 2 * NX * NY * NZ * 27 * C * C, bytes_accessed=4 * 2**20, transcendentals=0
        ),
    )(*[pltpu.with_memory_space_constraint(v, pltpu.HBM) for v in (features, cotangent, weights, ground, thick)])
    return pl.pallas_call(
        hand_on,
        out_shape=(block, block, jax.ShapeDtypeStruct((27, C, C), F32)),
        in_specs=[vmem] * 3,
        out_specs=(vmem,) * 3,
        compiler_params=pltpu.CompilerParams(vmem_limit_bytes=16 * 1024 * 1024),
    )(*results)


def solution(mesh):
    assert mesh.shape["gx"] == 16 and mesh.shape["gy"] == 8
    placed = (
        P(None, "gx", "gy", None),
        P(None, "gx", "gy", None),
        P(),
        P("gx", "gy"),
        P("gx", "gy"),
    )
    return jax.shard_map(
        shards,
        mesh=mesh,
        in_specs=placed,
        out_specs=(P(None, "gx", "gy", None), P(None, "gx", "gy", None), P()),
        check_vma=False,
    )
```

```python
import math

import jax
import jax.numpy as jnp
from jax import lax
from jax.experimental import pallas as pl
from jax.experimental.pallas import tpu as pltpu
from jax.sharding import PartitionSpec as P

MESH = pl.DeviceIdType.MESH
F32 = jnp.float32
BF16 = jnp.bfloat16
C = 96
NX, NY, NZ = 2, 8, 128
OWNERS = 14
BLOCK = 84
NEAR, FAR, SAME = 0, 1, 2
NT = (((1,), (1,)), ((), ()))


def kernel(
    scale,
    feat_hbm, cot_hbm, w_hbm, ground, thick,
    out, grad_in, full,
    feat, cot, w, pf, pc, tmp, shifted, lf, lb, red, core_box, late_box, mid_box, late_ring, mid_ring, tout,
    load_sem, halo_send, halo_recv, core_send, core_recv,
    rs_send, rs_recv, ag_send, ag_recv, ring_send, ring_recv, plane_sem,
):
    gx = lax.axis_index("gx")
    gy = lax.axis_index("gy")
    core = lax.rem(gx, 2)
    cx = lax.div(gx, 4)
    cy = lax.rem(lax.div(gx, 2), 2) * 2 + lax.rem(gy, 2)
    cz = lax.div(gy, 2)
    near_gx = gx + 1 - 2 * core
    far_gx = gx - 1 + 2 * core
    has_far = jnp.logical_and(far_gx >= 0, far_gx < 16)
    near_x = 1 - core
    far_x = core
    near_a = 2 * (1 - core)
    far_a = 2 * core

    loads = [
        pltpu.make_async_copy(feat_hbm, feat, load_sem.at[0]),
        pltpu.make_async_copy(cot_hbm, cot, load_sem.at[1]),
        pltpu.make_async_copy(w_hbm, w, load_sem.at[2]),
    ]
    for load in loads:
        load.start()

    def chip(x, y, z):
        return (x * 4 + lax.div(y, 2) * 2 + core, z * 2 + lax.rem(y, 2))

    def step(dx, dy, dz):
        return lax.rem(cx + dx, 4), lax.rem(cy + dy, 4), lax.rem(cz + dz, 4)

    has_dy = {-1: gy > 0, 0: None, 1: gy < 7}

    def present(side, dy):
        terms = []
        if side == FAR:
            terms.append(has_far)
        if dy != 0:
            terms.append(has_dy[dy])
        if not terms:
            return None
        return terms[0] if len(terms) == 1 else jnp.logical_and(*terms)

    def when(cond, fn):
        if cond is None:
            fn()
        else:
            pl.when(cond)(fn)

    def halo_device(side, dy):
        return ({NEAR: near_gx, FAR: far_gx, SAME: gx}[side], gy + dy)

    halos = [(SAME, -1), (SAME, 1), (FAR, 0), (FAR, -1), (FAR, 1), (NEAR, 0)]
    rings = {
        "x": [chip(*step(d, 0, 0)) for d in (1, 2, 3)],
        "y": [chip(*step(0, d, 0)) for d in (1, 2, 3)],
        "z": [chip(*step(0, 0, d)) for d in (1, 2, 3)],
    }

    def signal(sem, device):
        pl.semaphore_signal(sem, inc=1, device_id=device, device_id_type=MESH)

    barrier = pltpu.get_barrier_semaphore()
    for side, dy in halos:
        when(present(side, dy), lambda side=side, dy=dy: signal(barrier, halo_device(side, dy)))
    for axis in "xyz":
        for device in rings[axis]:
            signal(barrier, device)

    rows = lax.broadcasted_iota(jnp.int32, (NY, NZ), 0)
    heights = lax.broadcasted_iota(jnp.int32, (NY, NZ), 1)

    def occupied(x):
        low = jnp.zeros((NY, NZ), jnp.int32)
        high = jnp.zeros((NY, NZ), jnp.int32)
        for y in range(NY):
            g = ground[x, y]
            low = jnp.where(rows == y, g, low)
            high = jnp.where(rows == y, g + thick[x, y], high)
        return jnp.logical_and(heights >= low, heights < high)

    def columns(src, dst, x, shifts):
        value = jnp.where(occupied(x)[None], src[:, x].astype(F32), 0.0)
        tmp[...] = value.reshape(C * NY, NZ)
        for y in range(NY):
            col = tmp[pl.ds(y, C, stride=NY), :]
            dst[x + 1, y + 1] = col.astype(BF16)
            if shifts:
                lanes = slice(y * NZ, (y + 1) * NZ)
                shifted[x, 0:C, lanes] = pltpu.roll(col, NZ - 1, 1).astype(BF16)
                shifted[x, C : 2 * C, lanes] = col.astype(BF16)
                shifted[x, 2 * C : 3 * C, lanes] = pltpu.roll(col, 1, 1).astype(BF16)

    loads[0].wait()
    for x in range(NX):
        columns(feat, pf, x, False)

    n_dy = jnp.where(gy > 0, 1, 0) + jnp.where(gy < 7, 1, 0)
    n_far = jnp.where(has_far, 1, 0)
    pl.semaphore_wait(barrier, n_dy + n_far * (n_dy + 1) + 1 + 9)

    src_y = {-1: 1, 0: 1, 1: NY}
    dst_y = {-1: NY + 1, 0: 1, 1: 0}
    len_y = {-1: 1, 0: NY, 1: 1}

    def halo_copy(which, side, dy):
        buf = (pf, pc)[which]
        n = len_y[dy]
        if side == SAME:
            src_x = dst_x = pl.ds(1, 2)
        elif side == NEAR:
            src_x, dst_x = pl.ds(2 - core, 1), pl.ds(3 * core, 1)
        else:
            src_x, dst_x = pl.ds(1 + core, 1), pl.ds(3 * (1 - core), 1)
        return pltpu.make_async_remote_copy(
            src_ref=buf.at[src_x, pl.ds(src_y[dy], n)],
            dst_ref=buf.at[dst_x, pl.ds(dst_y[dy], n)],
            send_sem=halo_send.at[which, side, dy + 1],
            recv_sem=halo_recv.at[which, side, dy + 1],
            device_id=halo_device(side, dy),
            device_id_type=MESH,
        )

    def send_halos(which, sides=(SAME, FAR, NEAR)):
        for side, dy in halos:
            if side in sides:
                when(present(side, dy), lambda side=side, dy=dy: halo_copy(which, side, dy).start())

    def recv_halos(which, sides):
        for side, dy in halos:
            if side in sides:
                when(present(side, -dy), lambda side=side, dy=dy: halo_copy(which, side, dy).wait_recv())

    def done_halos(which, sides):
        for side, dy in halos:
            if side in sides:
                when(present(side, dy), lambda side=side, dy=dy: halo_copy(which, side, dy).wait_send())

    def corner_copy(which, e):
        buf = (pf, pc)[which]
        y = pl.ds(0 if e < 0 else NY + 1, 1)
        return pltpu.make_async_remote_copy(
            src_ref=buf.at[pl.ds(2 - core, 1), y],
            dst_ref=buf.at[pl.ds(3 * core, 1), y],
            send_sem=halo_send.at[which, NEAR, e + 1],
            recv_sem=halo_recv.at[which, NEAR, e + 1],
            device_id=(near_gx, gy),
            device_id_type=MESH,
        )

    def corners(which, act):
        for e in (-1, 1):
            pl.when(has_dy[e])(lambda e=e: act(corner_copy(which, e)))

    def clear_edges(buf):
        zeros = jnp.zeros((C, NZ), BF16)

        def far_side():
            for y in range(NY + 2):
                buf[3 * core, y] = zeros

        def y_side(y):
            for x in range(NX + 2):
                buf[x, y] = zeros

        pl.when(jnp.logical_not(has_far))(far_side)
        pl.when(gy == 0)(lambda: y_side(0))
        pl.when(gy == 7)(lambda: y_side(NY + 1))

    send_halos(0)
    for device in rings["z"]:
        signal(plane_sem, device)
    loads[1].wait()
    for x in range(NX):
        columns(cot, pc, x, True)
    send_halos(1, (SAME, NEAR))

    def weight_terms(xs, a, ys):
        lhs = jnp.concatenate([shifted[x, :, y * NZ : (y + 1) * NZ] for x in xs for y in ys], axis=1)
        rhs = jnp.concatenate(
            [jnp.concatenate([pf[x + a, y + b] for x in xs for y in ys], axis=1) for b in range(3)],
            axis=0,
        )
        return lax.dot_general(lhs, rhs, NT, preferred_element_type=F32)

    def put(a, value, add):
        rest = jnp.concatenate([value[72 * q : 72 * q + 72, 256:288] for q in range(4)], axis=1)
        parts = (
            (0, 36, value[:, 0:128]), (36, 36, value[:, 128:256]), (72, 9, rest),
        )
        for start, n, part in parts:
            at = pl.ds(BLOCK * a + start, n)
            part = part.reshape(n, 8, 128)
            red[at] = red[at] + part if add else part
        if not add:
            red[pl.ds(BLOCK * a + 81, 3)] = jnp.zeros((3, 8, 128), F32)

    def core_copy(k, src, dst):
        return pltpu.make_async_remote_copy(
            src_ref=src, dst_ref=dst, send_sem=core_send.at[k], recv_sem=core_recv.at[k],
            device_id=(near_gx, gy), device_id_type=MESH,
        )

    def late_part(buf, m):
        return buf.at[pl.ds(2 * BLOCK * m, BLOCK)]

    def mid_part(buf, m):
        return buf.at[pl.ds(BLOCK + BLOCK // 2 * m, BLOCK // 2)]

    other = 1 - core
    inner, outer, both = range(1, NY - 1), (0, NY - 1), (near_x, far_x)
    put(1, weight_terms(both, 1, inner), False)
    put(far_a, weight_terms((near_x,), far_a, inner), False)
    clear_edges(pf)
    clear_edges(pc)
    recv_halos(0, (NEAR,))
    put(near_a, weight_terms(both, near_a, inner), False)
    recv_halos(0, (SAME,))
    corners(0, lambda copy: copy.start())
    put(1, weight_terms(both, 1, outer), True)
    pairs = [core_copy(0, mid_part(red, other), core_box.at[pl.ds(BLOCK, BLOCK // 2)])]
    pairs[0].start()
    put(far_a, weight_terms((near_x,), far_a, outer), True)
    corners(0, lambda copy: copy.wait_recv())
    put(near_a, weight_terms(both, near_a, outer), True)
    pairs.append(core_copy(1, late_part(red, other), core_box.at[pl.ds(0, BLOCK)]))
    pairs[1].start()

    def conv_pair(x, j, buf, lhs):
        stack = jnp.concatenate(
            [
                jnp.concatenate([buf[x + a, 2 * j + b], buf[x + a, 2 * j + b + 1]], axis=1)
                for a in range(3)
                for b in range(3)
            ],
            axis=0,
        )
        prod = jnp.dot(lhs[...], stack, preferred_element_type=F32)
        for half in range(2):
            part = prod[:, half * NZ : (half + 1) * NZ]
            col = (
                pltpu.roll(part[0:C], 1, 1) + part[C : 2 * C] + pltpu.roll(part[2 * C : 3 * C], NZ - 1, 1)
            )
            tout[pl.ds(2 * j + half, C, stride=NY), :] = col

    def conv(x, buf, lhs, dst):
        for j in range(NY // 2):
            conv_pair(x, j, buf, lhs)
        mask = occupied(x)
        dst[:, x] = jnp.where(mask[None], tout[...].reshape(C, NY, NZ), 0.0).astype(BF16)

    me = cx * 4 + cz
    plane = sorted(
        [(dx, dz) for dx in range(4) for dz in range(4) if (dx, dz) != (0, 0)],
        key=lambda d: -sum(min(v, 4 - v) for v in d),
    )

    def late_share(buf, j):
        return buf.at[pl.ds(2 * BLOCK * core + 6 * j, 6)]

    def mid_share(buf, j):
        return buf.at[pl.ds(BLOCK + BLOCK // 2 * core + 3 * j, 3)]

    shares = (mid_share, late_share)
    boxes = (mid_box, late_box)
    circles = (mid_ring, late_ring)

    def exchange(index):
        for dx, dz in plane:
            x, y, z = step(dx, 0, dz)
            j = x * 4 + z

            @pl.when(j < OWNERS)
            def _(device=chip(x, y, z), j=j, d=dx * 4 + dz):
                pltpu.make_async_remote_copy(
                    src_ref=shares[index](red, j), dst_ref=boxes[index].at[d],
                    send_sem=rs_send.at[index], recv_sem=rs_recv.at[index],
                    device_id=device, device_id_type=MESH,
                ).start()

    def drain(ref, sem):
        pltpu.make_async_copy(ref, ref, sem).wait()

    def owner(fn):
        pl.when(me < OWNERS)(fn)

    def collect(index):
        @owner
        def _():
            drain(boxes[index].at[pl.ds(1, 15)], rs_recv.at[index])
            circles[index][cy] = shares[index](red, me)[...] + jnp.sum(boxes[index][1:16], axis=0)
            for device in rings["y"]:
                here = circles[index].at[cy]
                pltpu.make_async_remote_copy(
                    src_ref=here, dst_ref=here, send_sem=ring_send.at[index], recv_sem=ring_recv.at[index],
                    device_id=device, device_id_type=MESH,
                ).start()

    def hand_out(index, j, device, d):
        share = shares[index](full, j)
        return pltpu.make_async_remote_copy(
            src_ref=share, dst_ref=share, send_sem=ag_send.at[index], recv_sem=ag_recv.at[index, d],
            device_id=device, device_id_type=MESH,
        )

    def pass_on(index, j):
        share = shares[index](full, j)
        core_copy(2 + index, share, share).start()

    def finish(index):
        @owner
        def _():
            drain(circles[index].at[pl.ds(0, 3)], ring_recv.at[index])
            terms = [circles[index][y] for y in range(4)]
            shares[index](full, me)[...] = ((terms[0] + terms[1]) + (terms[2] + terms[3])) * scale
            for dx, dz in plane:
                hand_out(index, me, chip(*step(dx, 0, dz)), dx * 4 + dz).start()
            pass_on(index, me)

    def gather(index):
        for dx, dz in reversed(plane):
            x, y, z = step(4 - dx, 0, 4 - dz)
            j = x * 4 + z

            @pl.when(j < OWNERS)
            def _(device=chip(x, y, z), j=j, d=dx * 4 + dz):
                hand_out(index, j, device, d).wait_recv()
                pass_on(index, j)

    pl.semaphore_wait(plane_sem, 3)
    pairs[0].wait_recv()
    mid = mid_part(red, core)
    mid[...] = mid[...] + core_box[BLOCK : BLOCK + BLOCK // 2]
    exchange(0)
    pairs[1].wait_recv()
    late = late_part(red, core)
    late[...] = late[...] + core_box[0:BLOCK]
    recv_halos(0, (FAR,))
    send_halos(1, (FAR,))
    put(far_a, weight_terms((far_x,), far_a, range(NY)), True)
    exchange(1)
    loads[2].wait()
    for c in range(3):
        lf[c * C : (c + 1) * C, :] = jnp.concatenate([w[ab * 3 + c] for ab in range(9)], axis=1)
        lb[c * C : (c + 1) * C, :] = jnp.concatenate(
            [w[26 - (ab * 3 + c)].T for ab in range(9)], axis=1
        )
    conv(near_x, pf, lf, out)
    collect(0)
    conv(far_x, pf, lf, out)
    recv_halos(1, (SAME, NEAR))
    corners(1, lambda copy: copy.start())
    collect(1)
    finish(0)
    corners(1, lambda copy: copy.wait_recv())
    conv(near_x, pc, lb, grad_in)
    finish(1)
    recv_halos(1, (FAR,))
    conv(far_x, pc, lb, grad_in)
    gather(0)
    gather(1)
    for which in range(2):
        done_halos(which, (NEAR, SAME, FAR))
        corners(which, lambda copy: copy.wait_send())
    for copy in pairs:
        copy.wait_send()
    for index, box in enumerate(boxes):
        owner(lambda: drain(box.at[pl.ds(0, OWNERS - 1)], rs_send.at[index]))
        pl.when(me >= OWNERS)(lambda: drain(box.at[pl.ds(0, OWNERS)], rs_send.at[index]))
        owner(lambda: drain(circles[index].at[pl.ds(0, 3)], ring_send.at[index]))
        owner(lambda: drain(box.at[pl.ds(0, 15)], ag_send.at[index]))
    for index, part in enumerate((mid_part, late_part)):
        passed = part(full, other)
        core_copy(2 + index, passed, passed).wait()


def hand_on(a, b, c, x, y, z, unpacked, sem):
    copies = [
        pltpu.make_async_copy(a, x, sem.at[3]),
        pltpu.make_async_copy(b, y, sem.at[4]),
    ]
    for copy in copies:
        copy.start()
    for k in range(3):
        tiles = c[BLOCK * k : BLOCK * k + 81]
        left = tiles[0:36].reshape(3 * C, 128)
        right = tiles[36:72].reshape(3 * C, 128)
        rest = tiles[72:81].reshape(72, 128)
        rest = jnp.concatenate([rest[:, 32 * q : 32 * q + 32] for q in range(4)], axis=0)
        blocks = (
            left[:, 0:C],
            jnp.concatenate([left[:, C:128], right[:, 0:64]], axis=1),
            jnp.concatenate([right[:, 64:128], rest], axis=1),
        )
        for i, block in enumerate(blocks):
            unpacked[9 * k + 3 * i : 9 * k + 3 * i + 3] = block.reshape(3, C, C)
        part = pl.ds(9 * k, 9)
        copies.append(pltpu.make_async_copy(unpacked.at[part], z.at[part], sem.at[k]))
        copies[-1].start()
    for copy in copies:
        copy.wait()


def shards(features, cotangent, weights, ground, thick):
    voxels = NX * NY * NZ * lax.axis_size("gx") * lax.axis_size("gy")
    block = jax.ShapeDtypeStruct((C, NX, NY, NZ), BF16)
    hbm = pl.BlockSpec(memory_space=pltpu.HBM)
    vmem = pl.BlockSpec(memory_space=pltpu.VMEM)
    smem = pl.BlockSpec(memory_space=pltpu.SMEM)

    def body(*refs):
        kernel(1.0 / math.sqrt(voxels), *refs)

    dma = pltpu.SemaphoreType.DMA
    inner = pltpu.VMEM((C, NX, NY, NZ), BF16)
    results = pl.pallas_call(
        body,
        out_shape=(inner, inner, pltpu.VMEM((3 * BLOCK, 8, 128), F32)),
        in_specs=[hbm, hbm, hbm, smem, smem],
        out_specs=(vmem, vmem, vmem),
        scratch_shapes=[
            inner,
            inner,
            pltpu.VMEM((27, C, C), BF16),
            pltpu.VMEM((NX + 2, NY + 2, C, NZ), BF16),
            pltpu.VMEM((NX + 2, NY + 2, C, NZ), BF16),
            pltpu.VMEM((C * NY, NZ), F32),
            pltpu.VMEM((NX, 3 * C, NY * NZ), BF16),
            pltpu.VMEM((3 * C, 9 * C), BF16),
            pltpu.VMEM((3 * C, 9 * C), BF16),
            pltpu.VMEM((3 * BLOCK, 8, 128), F32),
            pltpu.VMEM((BLOCK + BLOCK // 2, 8, 128), F32),
            pltpu.VMEM((16, 6, 8, 128), F32),
            pltpu.VMEM((16, 3, 8, 128), F32),
            pltpu.VMEM((4, 6, 8, 128), F32),
            pltpu.VMEM((4, 3, 8, 128), F32),
            pltpu.VMEM((C * NY, NZ), F32),
            dma((3,)),
            dma((2, 3, 3)),
            dma((2, 3, 3)),
            dma((4,)),
            dma((4,)),
            dma((2,)),
            dma((2,)),
            dma((2,)),
            dma((2, 16)),
            dma((2,)),
            dma((2,)),
            pltpu.SemaphoreType.REGULAR,
        ],
        compiler_params=pltpu.CompilerParams(
            collective_id=0, has_side_effects=True, vmem_limit_bytes=48 * 1024 * 1024
        ),
        cost_estimate=pl.CostEstimate(
            flops=3 * 2 * NX * NY * NZ * 27 * C * C, bytes_accessed=4 * 2**20, transcendentals=0
        ),
    )(*[pltpu.with_memory_space_constraint(v, pltpu.HBM) for v in (features, cotangent, weights, ground, thick)])
    return pl.pallas_call(
        hand_on,
        out_shape=(block, block, jax.ShapeDtypeStruct((27, C, C), F32)),
        in_specs=[vmem] * 3,
        out_specs=(hbm,) * 3,
        scratch_shapes=[pltpu.VMEM((27, C, C), F32), dma((5,))],
        compiler_params=pltpu.CompilerParams(vmem_limit_bytes=16 * 1024 * 1024),
    )(*results)


def solution(mesh):
    assert mesh.shape["gx"] == 16 and mesh.shape["gy"] == 8
    placed = (
        P(None, "gx", "gy", None),
        P(None, "gx", "gy", None),
        P(),
        P("gx", "gy"),
        P("gx", "gy"),
    )
    return jax.shard_map(
        shards,
        mesh=mesh,
        in_specs=placed,
        out_specs=(P(None, "gx", "gy", None), P(None, "gx", "gy", None), P()),
        check_vma=False,
    )
```

```python
import math

import jax
import jax.numpy as jnp
from jax import lax
from jax.experimental import pallas as pl
from jax.experimental.pallas import tpu as pltpu
from jax.sharding import PartitionSpec as P

MESH = pl.DeviceIdType.MESH
F32 = jnp.float32
BF16 = jnp.bfloat16
C = 96
NX, NY, NZ = 2, 8, 128
OWNERS = 14
BLOCK = 84
STREAM = 42
NEAR, FAR, SAME = 0, 1, 2
NT = (((1,), (1,)), ((), ()))


def kernel(
    scale,
    feat_hbm, cot_hbm, w_hbm, ground_hbm, thick_hbm,
    out, grad_in, full,
    feat, cot, w, ground, thick, pf, pc, tmp, shifted, lf, lb, red, core_box, box, ring, tout,
    load_sem, halo_send, halo_recv, core_send, core_recv,
    rs_send, rs_recv, ag_send, ag_recv, ring_send, ring_recv, plane_sem,
):
    gx = lax.axis_index("gx")
    gy = lax.axis_index("gy")
    core = lax.rem(gx, 2)
    cx = lax.div(gx, 4)
    cy = lax.rem(lax.div(gx, 2), 2) * 2 + lax.rem(gy, 2)
    cz = lax.div(gy, 2)
    near_gx = gx + 1 - 2 * core
    far_gx = gx - 1 + 2 * core
    has_far = jnp.logical_and(far_gx >= 0, far_gx < 16)
    near_x = 1 - core
    far_x = core
    near_a = 2 * (1 - core)
    far_a = 2 * core

    loads = [
        pltpu.make_async_copy(feat_hbm, feat, load_sem.at[0]),
        pltpu.make_async_copy(cot_hbm, cot, load_sem.at[1]),
        pltpu.make_async_copy(w_hbm, w, load_sem.at[2]),
        pltpu.make_async_copy(ground_hbm, ground, load_sem.at[3]),
        pltpu.make_async_copy(thick_hbm, thick, load_sem.at[4]),
    ]
    for load in loads:
        load.start()

    def chip(x, y, z):
        return (x * 4 + lax.div(y, 2) * 2 + core, z * 2 + lax.rem(y, 2))

    def step(dx, dy, dz):
        return lax.rem(cx + dx, 4), lax.rem(cy + dy, 4), lax.rem(cz + dz, 4)

    has_dy = {-1: gy > 0, 0: None, 1: gy < 7}

    def present(side, dy):
        terms = []
        if side == FAR:
            terms.append(has_far)
        if dy != 0:
            terms.append(has_dy[dy])
        if not terms:
            return None
        return terms[0] if len(terms) == 1 else jnp.logical_and(*terms)

    def when(cond, fn):
        if cond is None:
            fn()
        else:
            pl.when(cond)(fn)

    def halo_device(side, dy):
        return ({NEAR: near_gx, FAR: far_gx, SAME: gx}[side], gy + dy)

    halos = [(SAME, -1), (SAME, 1), (FAR, 0), (FAR, -1), (FAR, 1), (NEAR, 0)]
    rings = {
        "x": [chip(*step(d, 0, 0)) for d in (1, 2, 3)],
        "y": [chip(*step(0, d, 0)) for d in (1, 2, 3)],
        "z": [chip(*step(0, 0, d)) for d in (1, 2, 3)],
    }

    def signal(sem, device):
        pl.semaphore_signal(sem, inc=1, device_id=device, device_id_type=MESH)

    barrier = pltpu.get_barrier_semaphore()
    for side, dy in halos:
        when(present(side, dy), lambda side=side, dy=dy: signal(barrier, halo_device(side, dy)))
    for axis in "xyz":
        for device in rings[axis]:
            signal(barrier, device)

    rows = lax.broadcasted_iota(jnp.int32, (NY, NZ), 0)
    heights = lax.broadcasted_iota(jnp.int32, (NY, NZ), 1)

    def occupied(x):
        low = jnp.zeros((NY, NZ), jnp.int32)
        high = jnp.zeros((NY, NZ), jnp.int32)
        for y in range(NY):
            g = ground[x, y]
            low = jnp.where(rows == y, g, low)
            high = jnp.where(rows == y, g + thick[x, y], high)
        return jnp.logical_and(heights >= low, heights < high)

    def columns(src, dst, x, shifts):
        value = jnp.where(occupied(x)[None], src[:, x].astype(F32), 0.0)
        tmp[...] = value.reshape(C * NY, NZ)
        for y in range(NY):
            col = tmp[pl.ds(y, C, stride=NY), :]
            dst[x + 1, y + 1] = col.astype(BF16)
            if shifts:
                lanes = slice(y * NZ, (y + 1) * NZ)
                shifted[x, 0:C, lanes] = pltpu.roll(col, NZ - 1, 1).astype(BF16)
                shifted[x, C : 2 * C, lanes] = col.astype(BF16)
                shifted[x, 2 * C : 3 * C, lanes] = pltpu.roll(col, 1, 1).astype(BF16)

    loads[3].wait()
    loads[4].wait()
    loads[0].wait()
    for x in range(NX):
        columns(feat, pf, x, False)

    n_dy = jnp.where(gy > 0, 1, 0) + jnp.where(gy < 7, 1, 0)
    n_far = jnp.where(has_far, 1, 0)
    pl.semaphore_wait(barrier, n_dy + n_far * (n_dy + 1) + 1 + 9)

    src_y = {-1: 1, 0: 1, 1: NY}
    dst_y = {-1: NY + 1, 0: 1, 1: 0}
    len_y = {-1: 1, 0: NY, 1: 1}

    def halo_copy(which, side, dy):
        buf = (pf, pc)[which]
        n = len_y[dy]
        if side == SAME:
            src_x = dst_x = pl.ds(1, 2)
        elif side == NEAR:
            src_x, dst_x = pl.ds(2 - core, 1), pl.ds(3 * core, 1)
        else:
            src_x, dst_x = pl.ds(1 + core, 1), pl.ds(3 * (1 - core), 1)
        return pltpu.make_async_remote_copy(
            src_ref=buf.at[src_x, pl.ds(src_y[dy], n)],
            dst_ref=buf.at[dst_x, pl.ds(dst_y[dy], n)],
            send_sem=halo_send.at[which, side, dy + 1],
            recv_sem=halo_recv.at[which, side, dy + 1],
            device_id=halo_device(side, dy),
            device_id_type=MESH,
        )

    def send_halos(which, sides=(SAME, FAR, NEAR)):
        for side, dy in halos:
            if side in sides:
                when(present(side, dy), lambda side=side, dy=dy: halo_copy(which, side, dy).start())

    def recv_halos(which, sides):
        for side, dy in halos:
            if side in sides:
                when(present(side, -dy), lambda side=side, dy=dy: halo_copy(which, side, dy).wait_recv())

    def done_halos(which, sides):
        for side, dy in halos:
            if side in sides:
                when(present(side, dy), lambda side=side, dy=dy: halo_copy(which, side, dy).wait_send())

    def corner_copy(which, e):
        buf = (pf, pc)[which]
        y = pl.ds(0 if e < 0 else NY + 1, 1)
        return pltpu.make_async_remote_copy(
            src_ref=buf.at[pl.ds(2 - core, 1), y],
            dst_ref=buf.at[pl.ds(3 * core, 1), y],
            send_sem=halo_send.at[which, NEAR, e + 1],
            recv_sem=halo_recv.at[which, NEAR, e + 1],
            device_id=(near_gx, gy),
            device_id_type=MESH,
        )

    def corners(which, act):
        for e in (-1, 1):
            pl.when(has_dy[e])(lambda e=e: act(corner_copy(which, e)))

    def clear_edges(buf):
        zeros = jnp.zeros((C, NZ), BF16)

        def far_side():
            for y in range(NY + 2):
                buf[3 * core, y] = zeros

        def y_side(y):
            for x in range(NX + 2):
                buf[x, y] = zeros

        pl.when(jnp.logical_not(has_far))(far_side)
        pl.when(gy == 0)(lambda: y_side(0))
        pl.when(gy == 7)(lambda: y_side(NY + 1))

    send_halos(0)
    for device in rings["z"]:
        signal(plane_sem, device)
    loads[1].wait()
    for x in range(NX):
        columns(cot, pc, x, True)
    send_halos(1, (SAME, NEAR))

    def weight_terms(xs, a, ys):
        lhs = jnp.concatenate([shifted[x, :, y * NZ : (y + 1) * NZ] for x in xs for y in ys], axis=1)
        rhs = jnp.concatenate(
            [jnp.concatenate([pf[x + a, y + b] for x in xs for y in ys], axis=1) for b in range(3)],
            axis=0,
        )
        return lax.dot_general(lhs, rhs, NT, preferred_element_type=F32)

    def put(a, value, add):
        rest = jnp.concatenate([value[72 * q : 72 * q + 72, 256:288] for q in range(4)], axis=1)
        parts = (
            (0, 36, value[:, 0:128]), (36, 36, value[:, 128:256]), (72, 9, rest),
        )
        for start, n, part in parts:
            at = pl.ds(BLOCK * a + start, n)
            part = part.reshape(n, 8, 128)
            red[at] = red[at] + part if add else part
        if not add:
            red[pl.ds(BLOCK * a + 81, 3)] = jnp.zeros((3, 8, 128), F32)

    def core_copy(k, src, dst):
        return pltpu.make_async_remote_copy(
            src_ref=src, dst_ref=dst, send_sem=core_send.at[k], recv_sem=core_recv.at[k],
            device_id=(near_gx, gy), device_id_type=MESH,
        )

    def late_part(buf, m):
        return buf.at[pl.ds(2 * BLOCK * m, BLOCK)]

    def mid_part(buf, m):
        return buf.at[pl.ds(BLOCK + STREAM * m, STREAM)]

    other = 1 - core
    inner, outer, both = range(1, NY - 1), (0, NY - 1), (near_x, far_x)
    put(1, weight_terms(both, 1, inner), False)
    put(far_a, weight_terms((near_x,), far_a, inner), False)
    clear_edges(pf)
    clear_edges(pc)
    recv_halos(0, (NEAR,))
    put(near_a, weight_terms(both, near_a, inner), False)
    recv_halos(0, (SAME,))
    corners(0, lambda copy: copy.start())
    put(1, weight_terms(both, 1, outer), True)
    pairs = [core_copy(0, mid_part(red, other), core_box.at[pl.ds(BLOCK, STREAM)])]
    pairs[0].start()
    put(far_a, weight_terms((near_x,), far_a, outer), True)
    corners(0, lambda copy: copy.wait_recv())
    put(near_a, weight_terms(both, near_a, outer), True)
    pairs.append(core_copy(1, late_part(red, other), core_box.at[pl.ds(0, BLOCK)]))
    pairs[1].start()

    def conv_pair(x, j, buf, lhs):
        stack = jnp.concatenate(
            [
                jnp.concatenate([buf[x + a, 2 * j + b], buf[x + a, 2 * j + b + 1]], axis=1)
                for a in range(3)
                for b in range(3)
            ],
            axis=0,
        )
        prod = jnp.dot(lhs[...], stack, preferred_element_type=F32)
        for half in range(2):
            part = prod[:, half * NZ : (half + 1) * NZ]
            col = (
                pltpu.roll(part[0:C], 1, 1) + part[C : 2 * C] + pltpu.roll(part[2 * C : 3 * C], NZ - 1, 1)
            )
            tout[pl.ds(2 * j + half, C, stride=NY), :] = col

    def conv(x, buf, lhs, dst):
        for j in range(NY // 2):
            conv_pair(x, j, buf, lhs)
        mask = occupied(x)
        dst[:, x] = jnp.where(mask[None], tout[...].reshape(C, NY, NZ), 0.0).astype(BF16)

    me = cx * 4 + cz
    plane = sorted(
        [(dx, dz) for dx in range(4) for dz in range(4) if (dx, dz) != (0, 0)],
        key=lambda d: -sum(min(v, 4 - v) for v in d),
    )

    def stream(base):
        return lambda buf, j: buf.at[pl.ds(base + 3 * j, 3)]

    shares = [stream(BLOCK + STREAM * core), stream(2 * BLOCK * core), stream(2 * BLOCK * core + STREAM)]
    boxes = [box.at[i] for i in range(3)]
    circles = [ring.at[i] for i in range(3)]

    def exchange(index):
        for dx, dz in plane:
            x, y, z = step(dx, 0, dz)
            j = x * 4 + z

            @pl.when(j < OWNERS)
            def _(device=chip(x, y, z), j=j, d=dx * 4 + dz):
                pltpu.make_async_remote_copy(
                    src_ref=shares[index](red, j), dst_ref=boxes[index].at[d],
                    send_sem=rs_send.at[index], recv_sem=rs_recv.at[index],
                    device_id=device, device_id_type=MESH,
                ).start()

    def drain(ref, sem):
        pltpu.make_async_copy(ref, ref, sem).wait()

    def owner(fn):
        pl.when(me < OWNERS)(fn)

    def collect(index):
        @owner
        def _():
            drain(boxes[index].at[pl.ds(1, 15)], rs_recv.at[index])
            circles[index][cy] = shares[index](red, me)[...] + jnp.sum(boxes[index][1:16], axis=0)
            for device in rings["y"]:
                here = circles[index].at[cy]
                pltpu.make_async_remote_copy(
                    src_ref=here, dst_ref=here, send_sem=ring_send.at[index], recv_sem=ring_recv.at[index],
                    device_id=device, device_id_type=MESH,
                ).start()

    def hand_out(index, j, device, d):
        share = shares[index](full, j)
        return pltpu.make_async_remote_copy(
            src_ref=share, dst_ref=share, send_sem=ag_send.at[index], recv_sem=ag_recv.at[index, d],
            device_id=device, device_id_type=MESH,
        )

    def pass_on(index, j):
        share = shares[index](full, j)
        core_copy(min(2 + index, 3), share, share).start()

    def finish(index):
        @owner
        def _():
            drain(circles[index].at[pl.ds(0, 3)], ring_recv.at[index])
            terms = [circles[index][y] for y in range(4)]
            shares[index](full, me)[...] = ((terms[0] + terms[1]) + (terms[2] + terms[3])) * scale
            for dx, dz in plane:
                hand_out(index, me, chip(*step(dx, 0, dz)), dx * 4 + dz).start()
            pass_on(index, me)

    def gather(index):
        for dx, dz in reversed(plane):
            x, y, z = step(4 - dx, 0, 4 - dz)
            j = x * 4 + z

            @pl.when(j < OWNERS)
            def _(device=chip(x, y, z), j=j, d=dx * 4 + dz):
                hand_out(index, j, device, d).wait_recv()
                pass_on(index, j)

    pl.semaphore_wait(plane_sem, 3)
    pairs[0].wait_recv()
    mid = mid_part(red, core)
    mid[...] = mid[...] + core_box[BLOCK : BLOCK + STREAM]
    exchange(0)
    pairs[1].wait_recv()
    late = late_part(red, core)
    late[...] = late[...] + core_box[0:BLOCK]
    recv_halos(0, (FAR,))
    send_halos(1, (FAR,))
    put(far_a, weight_terms((far_x,), far_a, range(NY)), True)
    exchange(1)
    exchange(2)
    loads[2].wait()
    for c in range(3):
        lf[c * C : (c + 1) * C, :] = jnp.concatenate([w[ab * 3 + c] for ab in range(9)], axis=1)
        lb[c * C : (c + 1) * C, :] = jnp.concatenate(
            [w[26 - (ab * 3 + c)].T for ab in range(9)], axis=1
        )
    conv(near_x, pf, lf, out)
    collect(0)
    conv(far_x, pf, lf, out)
    recv_halos(1, (SAME, NEAR))
    corners(1, lambda copy: copy.start())
    collect(1)
    collect(2)
    finish(0)
    corners(1, lambda copy: copy.wait_recv())
    conv(near_x, pc, lb, grad_in)
    finish(1)
    finish(2)
    gather(0)
    recv_halos(1, (FAR,))
    conv(far_x, pc, lb, grad_in)
    gather(1)
    gather(2)
    for which in range(2):
        done_halos(which, (NEAR, SAME, FAR))
        corners(which, lambda copy: copy.wait_send())
    for copy in pairs:
        copy.wait_send()
    for index, slots in enumerate(boxes):
        owner(lambda: drain(slots.at[pl.ds(0, OWNERS - 1)], rs_send.at[index]))
        pl.when(me >= OWNERS)(lambda: drain(slots.at[pl.ds(0, OWNERS)], rs_send.at[index]))
        owner(lambda: drain(circles[index].at[pl.ds(0, 3)], ring_send.at[index]))
        owner(lambda: drain(slots.at[pl.ds(0, 15)], ag_send.at[index]))
    for index, part in enumerate((mid_part, late_part)):
        passed = part(full, other)
        core_copy(2 + index, passed, passed).wait()


def hand_on(a, b, c, x, y, z, unpacked, sem):
    copies = [
        pltpu.make_async_copy(a, x, sem.at[3]),
        pltpu.make_async_copy(b, y, sem.at[4]),
    ]
    for copy in copies:
        copy.start()
    for k in range(3):
        tiles = c[BLOCK * k : BLOCK * k + 81]
        left = tiles[0:36].reshape(3 * C, 128)
        right = tiles[36:72].reshape(3 * C, 128)
        rest = tiles[72:81].reshape(72, 128)
        rest = jnp.concatenate([rest[:, 32 * q : 32 * q + 32] for q in range(4)], axis=0)
        blocks = (
            left[:, 0:C],
            jnp.concatenate([left[:, C:128], right[:, 0:64]], axis=1),
            jnp.concatenate([right[:, 64:128], rest], axis=1),
        )
        for i, block in enumerate(blocks):
            unpacked[9 * k + 3 * i : 9 * k + 3 * i + 3] = block.reshape(3, C, C)
        part = pl.ds(9 * k, 9)
        copies.append(pltpu.make_async_copy(unpacked.at[part], z.at[part], sem.at[k]))
        copies[-1].start()
    for copy in copies:
        copy.wait()


def shards(features, cotangent, weights, ground, thick):
    voxels = NX * NY * NZ * lax.axis_size("gx") * lax.axis_size("gy")
    block = jax.ShapeDtypeStruct((C, NX, NY, NZ), BF16)
    hbm = pl.BlockSpec(memory_space=pltpu.HBM)
    vmem = pl.BlockSpec(memory_space=pltpu.VMEM)

    def body(*refs):
        kernel(1.0 / math.sqrt(voxels), *refs)

    dma = pltpu.SemaphoreType.DMA
    inner = pltpu.VMEM((C, NX, NY, NZ), BF16)
    results = pl.pallas_call(
        body,
        out_shape=(inner, inner, pltpu.VMEM((3 * BLOCK, 8, 128), F32)),
        in_specs=[hbm] * 5,
        out_specs=(vmem, vmem, vmem),
        scratch_shapes=[
            inner,
            inner,
            pltpu.VMEM((27, C, C), BF16),
            pltpu.SMEM((NX, NY), jnp.int32),
            pltpu.SMEM((NX, NY), jnp.int32),
            pltpu.VMEM((NX + 2, NY + 2, C, NZ), BF16),
            pltpu.VMEM((NX + 2, NY + 2, C, NZ), BF16),
            pltpu.VMEM((C * NY, NZ), F32),
            pltpu.VMEM((NX, 3 * C, NY * NZ), BF16),
            pltpu.VMEM((3 * C, 9 * C), BF16),
            pltpu.VMEM((3 * C, 9 * C), BF16),
            pltpu.VMEM((3 * BLOCK, 8, 128), F32),
            pltpu.VMEM((BLOCK + STREAM, 8, 128), F32),
            pltpu.VMEM((3, 16, 3, 8, 128), F32),
            pltpu.VMEM((3, 4, 3, 8, 128), F32),
            pltpu.VMEM((C * NY, NZ), F32),
            dma((5,)),
            dma((2, 3, 3)),
            dma((2, 3, 3)),
            dma((4,)),
            dma((4,)),
            dma((3,)),
            dma((3,)),
            dma((3,)),
            dma((3, 16)),
            dma((3,)),
            dma((3,)),
            pltpu.SemaphoreType.REGULAR,
        ],
        compiler_params=pltpu.CompilerParams(
            collective_id=0, has_side_effects=True, vmem_limit_bytes=48 * 1024 * 1024
        ),
        cost_estimate=pl.CostEstimate(
            flops=3 * 2 * NX * NY * NZ * 27 * C * C, bytes_accessed=4 * 2**20, transcendentals=0
        ),
    )(*[pltpu.with_memory_space_constraint(v, pltpu.HBM) for v in (features, cotangent, weights, ground, thick)])
    return pl.pallas_call(
        hand_on,
        out_shape=(block, block, jax.ShapeDtypeStruct((27, C, C), F32)),
        in_specs=[vmem] * 3,
        out_specs=(hbm,) * 3,
        scratch_shapes=[pltpu.VMEM((27, C, C), F32), dma((5,))],
        compiler_params=pltpu.CompilerParams(vmem_limit_bytes=16 * 1024 * 1024),
    )(*results)


def solution(mesh):
    assert mesh.shape["gx"] == 16 and mesh.shape["gy"] == 8
    placed = (
        P(None, "gx", "gy", None),
        P(None, "gx", "gy", None),
        P(),
        P("gx", "gy"),
        P("gx", "gy"),
    )
    return jax.shard_map(
        shards,
        mesh=mesh,
        in_specs=placed,
        out_specs=(P(None, "gx", "gy", None), P(None, "gx", "gy", None), P()),
        check_vma=False,
    )
```

```python
import math

import jax
import jax.numpy as jnp
from jax import lax
from jax.experimental import pallas as pl
from jax.experimental.pallas import tpu as pltpu
from jax.sharding import PartitionSpec as P

MESH = pl.DeviceIdType.MESH
F32 = jnp.float32
BF16 = jnp.bfloat16
C = 96
NX, NY, NZ = 2, 8, 128
OWNERS = 14
BLOCK = 84
STREAM = 42
NEAR, FAR, SAME = 0, 1, 2
NT = (((1,), (1,)), ((), ()))


def kernel(
    scale,
    feat_hbm, cot_hbm, w_hbm, ground_hbm, thick_hbm,
    out, grad_in, full,
    feat, cot, w, ground, thick, pf, pc, tmp, shifted, lf, lb, red, core_box, mid_box, late_box, mid_ring, late_ring, tout,
    load_sem, halo_send, halo_recv, core_send, core_recv,
    rs_send, rs_recv, ag_send, ag_recv, ring_send, ring_recv, plane_sem,
):
    gx = lax.axis_index("gx")
    gy = lax.axis_index("gy")
    core = lax.rem(gx, 2)
    cx = lax.div(gx, 4)
    cy = lax.rem(lax.div(gx, 2), 2) * 2 + lax.rem(gy, 2)
    cz = lax.div(gy, 2)
    near_gx = gx + 1 - 2 * core
    far_gx = gx - 1 + 2 * core
    has_far = jnp.logical_and(far_gx >= 0, far_gx < 16)
    near_x = 1 - core
    far_x = core
    near_a = 2 * (1 - core)
    far_a = 2 * core

    loads = [
        pltpu.make_async_copy(feat_hbm, feat, load_sem.at[0]),
        pltpu.make_async_copy(cot_hbm, cot, load_sem.at[1]),
        pltpu.make_async_copy(w_hbm, w, load_sem.at[2]),
        pltpu.make_async_copy(ground_hbm, ground, load_sem.at[3]),
        pltpu.make_async_copy(thick_hbm, thick, load_sem.at[4]),
    ]
    for load in loads:
        load.start()

    def chip(x, y, z):
        return (x * 4 + lax.div(y, 2) * 2 + core, z * 2 + lax.rem(y, 2))

    def step(dx, dy, dz):
        return lax.rem(cx + dx, 4), lax.rem(cy + dy, 4), lax.rem(cz + dz, 4)

    has_dy = {-1: gy > 0, 0: None, 1: gy < 7}

    def present(side, dy):
        terms = []
        if side == FAR:
            terms.append(has_far)
        if dy != 0:
            terms.append(has_dy[dy])
        if not terms:
            return None
        return terms[0] if len(terms) == 1 else jnp.logical_and(*terms)

    def when(cond, fn):
        if cond is None:
            fn()
        else:
            pl.when(cond)(fn)

    def halo_device(side, dy):
        return ({NEAR: near_gx, FAR: far_gx, SAME: gx}[side], gy + dy)

    halos = [(SAME, -1), (SAME, 1), (FAR, 0), (FAR, -1), (FAR, 1), (NEAR, 0)]
    rings = {
        "x": [chip(*step(d, 0, 0)) for d in (1, 2, 3)],
        "y": [chip(*step(0, d, 0)) for d in (1, 2, 3)],
        "z": [chip(*step(0, 0, d)) for d in (1, 2, 3)],
    }

    def signal(sem, device):
        pl.semaphore_signal(sem, inc=1, device_id=device, device_id_type=MESH)

    barrier = pltpu.get_barrier_semaphore()
    for side, dy in halos:
        when(present(side, dy), lambda side=side, dy=dy: signal(barrier, halo_device(side, dy)))
    for axis in "xyz":
        for device in rings[axis]:
            signal(barrier, device)

    rows = lax.broadcasted_iota(jnp.int32, (NY, NZ), 0)
    heights = lax.broadcasted_iota(jnp.int32, (NY, NZ), 1)

    def occupied(x):
        low = jnp.zeros((NY, NZ), jnp.int32)
        high = jnp.zeros((NY, NZ), jnp.int32)
        for y in range(NY):
            g = ground[x, y]
            low = jnp.where(rows == y, g, low)
            high = jnp.where(rows == y, g + thick[x, y], high)
        return jnp.logical_and(heights >= low, heights < high)

    def columns(src, dst, x, shifts):
        value = jnp.where(occupied(x)[None], src[:, x].astype(F32), 0.0)
        tmp[...] = value.reshape(C * NY, NZ)
        for y in range(NY):
            col = tmp[pl.ds(y, C, stride=NY), :]
            dst[x + 1, y + 1] = col.astype(BF16)
            if shifts:
                lanes = slice(y * NZ, (y + 1) * NZ)
                shifted[x, 0:C, lanes] = pltpu.roll(col, NZ - 1, 1).astype(BF16)
                shifted[x, C : 2 * C, lanes] = col.astype(BF16)
                shifted[x, 2 * C : 3 * C, lanes] = pltpu.roll(col, 1, 1).astype(BF16)

    loads[3].wait()
    loads[4].wait()
    loads[0].wait()
    for x in range(NX):
        columns(feat, pf, x, False)

    n_dy = jnp.where(gy > 0, 1, 0) + jnp.where(gy < 7, 1, 0)
    n_far = jnp.where(has_far, 1, 0)
    pl.semaphore_wait(barrier, n_dy + n_far * (n_dy + 1) + 1 + 9)

    src_y = {-1: 1, 0: 1, 1: NY}
    dst_y = {-1: NY + 1, 0: 1, 1: 0}
    len_y = {-1: 1, 0: NY, 1: 1}

    def halo_copy(which, side, dy):
        buf = (pf, pc)[which]
        n = len_y[dy]
        if side == SAME:
            src_x = dst_x = pl.ds(1, 2)
        elif side == NEAR:
            src_x, dst_x = pl.ds(2 - core, 1), pl.ds(3 * core, 1)
        else:
            src_x, dst_x = pl.ds(1 + core, 1), pl.ds(3 * (1 - core), 1)
        return pltpu.make_async_remote_copy(
            src_ref=buf.at[src_x, pl.ds(src_y[dy], n)],
            dst_ref=buf.at[dst_x, pl.ds(dst_y[dy], n)],
            send_sem=halo_send.at[which, side, dy + 1],
            recv_sem=halo_recv.at[which, side, dy + 1],
            device_id=halo_device(side, dy),
            device_id_type=MESH,
        )

    def send_halos(which, sides=(SAME, FAR, NEAR)):
        for side, dy in halos:
            if side in sides:
                when(present(side, dy), lambda side=side, dy=dy: halo_copy(which, side, dy).start())

    def recv_halos(which, sides):
        for side, dy in halos:
            if side in sides:
                when(present(side, -dy), lambda side=side, dy=dy: halo_copy(which, side, dy).wait_recv())

    def done_halos(which, sides):
        for side, dy in halos:
            if side in sides:
                when(present(side, dy), lambda side=side, dy=dy: halo_copy(which, side, dy).wait_send())

    def corner_copy(which, e):
        buf = (pf, pc)[which]
        y = pl.ds(0 if e < 0 else NY + 1, 1)
        return pltpu.make_async_remote_copy(
            src_ref=buf.at[pl.ds(2 - core, 1), y],
            dst_ref=buf.at[pl.ds(3 * core, 1), y],
            send_sem=halo_send.at[which, NEAR, e + 1],
            recv_sem=halo_recv.at[which, NEAR, e + 1],
            device_id=(near_gx, gy),
            device_id_type=MESH,
        )

    def corners(which, act):
        for e in (-1, 1):
            pl.when(has_dy[e])(lambda e=e: act(corner_copy(which, e)))

    def clear_edges(buf):
        zeros = jnp.zeros((C, NZ), BF16)

        def far_side():
            for y in range(NY + 2):
                buf[3 * core, y] = zeros

        def y_side(y):
            for x in range(NX + 2):
                buf[x, y] = zeros

        pl.when(jnp.logical_not(has_far))(far_side)
        pl.when(gy == 0)(lambda: y_side(0))
        pl.when(gy == 7)(lambda: y_side(NY + 1))

    send_halos(0)
    for device in rings["z"]:
        signal(plane_sem, device)
    loads[1].wait()
    for x in range(NX):
        columns(cot, pc, x, True)
    send_halos(1, (SAME, NEAR))

    def weight_terms(xs, a, ys):
        lhs = jnp.concatenate([shifted[x, :, y * NZ : (y + 1) * NZ] for x in xs for y in ys], axis=1)
        rhs = jnp.concatenate(
            [jnp.concatenate([pf[x + a, y + b] for x in xs for y in ys], axis=1) for b in range(3)],
            axis=0,
        )
        return lax.dot_general(lhs, rhs, NT, preferred_element_type=F32)

    def put(a, value, add):
        rest = jnp.concatenate([value[72 * q : 72 * q + 72, 256:288] for q in range(4)], axis=1)
        parts = (
            (0, 36, value[:, 0:128]), (36, 36, value[:, 128:256]), (72, 9, rest),
        )
        for start, n, part in parts:
            at = pl.ds(BLOCK * a + start, n)
            part = part.reshape(n, 8, 128)
            red[at] = red[at] + part if add else part
        if not add:
            red[pl.ds(BLOCK * a + 81, 3)] = jnp.zeros((3, 8, 128), F32)

    def core_copy(k, src, dst):
        return pltpu.make_async_remote_copy(
            src_ref=src, dst_ref=dst, send_sem=core_send.at[k], recv_sem=core_recv.at[k],
            device_id=(near_gx, gy), device_id_type=MESH,
        )

    def late_part(buf, m):
        return buf.at[pl.ds(2 * BLOCK * m, BLOCK)]

    def mid_part(buf, m):
        return buf.at[pl.ds(BLOCK + STREAM * m, STREAM)]

    other = 1 - core
    inner, outer, both = range(1, NY - 1), (0, NY - 1), (near_x, far_x)
    put(1, weight_terms(both, 1, inner), False)
    put(far_a, weight_terms((near_x,), far_a, inner), False)
    clear_edges(pf)
    clear_edges(pc)
    recv_halos(0, (NEAR,))
    put(near_a, weight_terms(both, near_a, inner), False)
    recv_halos(0, (SAME,))
    corners(0, lambda copy: copy.start())
    put(1, weight_terms(both, 1, outer), True)
    pairs = [core_copy(0, mid_part(red, other), core_box.at[pl.ds(BLOCK, STREAM)])]
    pairs[0].start()
    put(far_a, weight_terms((near_x,), far_a, outer), True)
    corners(0, lambda copy: copy.wait_recv())
    put(near_a, weight_terms(both, near_a, outer), True)
    pairs.append(core_copy(1, late_part(red, other), core_box.at[pl.ds(0, BLOCK)]))
    pairs[1].start()

    def conv_pair(x, j, buf, lhs):
        stack = jnp.concatenate(
            [
                jnp.concatenate([buf[x + a, 2 * j + b], buf[x + a, 2 * j + b + 1]], axis=1)
                for a in range(3)
                for b in range(3)
            ],
            axis=0,
        )
        prod = jnp.dot(lhs[...], stack, preferred_element_type=F32)
        for half in range(2):
            part = prod[:, half * NZ : (half + 1) * NZ]
            col = (
                pltpu.roll(part[0:C], 1, 1) + part[C : 2 * C] + pltpu.roll(part[2 * C : 3 * C], NZ - 1, 1)
            )
            tout[pl.ds(2 * j + half, C, stride=NY), :] = col

    def conv(x, buf, lhs, dst):
        for j in range(NY // 2):
            conv_pair(x, j, buf, lhs)
        mask = occupied(x)
        dst[:, x] = jnp.where(mask[None], tout[...].reshape(C, NY, NZ), 0.0).astype(BF16)

    me = cx * 4 + cz
    plane = sorted(
        [(dx, dz) for dx in range(4) for dz in range(4) if (dx, dz) != (0, 0)],
        key=lambda d: -sum(min(v, 4 - v) for v in d),
    )

    def stream(base, n):
        return lambda buf, j: buf.at[pl.ds(base + n * j, n)]

    shares = [stream(BLOCK + STREAM * core, 3)]
    shares += [stream(2 * BLOCK * core + 2 * OWNERS * i, 2) for i in range(3)]
    boxes = [mid_box] + [late_box.at[i] for i in range(3)]
    circles = [mid_ring] + [late_ring.at[i] for i in range(3)]

    def exchange(index):
        for dx, dz in plane:
            x, y, z = step(dx, 0, dz)
            j = x * 4 + z

            @pl.when(j < OWNERS)
            def _(device=chip(x, y, z), j=j, d=dx * 4 + dz):
                pltpu.make_async_remote_copy(
                    src_ref=shares[index](red, j), dst_ref=boxes[index].at[d],
                    send_sem=rs_send.at[index], recv_sem=rs_recv.at[index],
                    device_id=device, device_id_type=MESH,
                ).start()

    def drain(ref, sem):
        pltpu.make_async_copy(ref, ref, sem).wait()

    def owner(fn):
        pl.when(me < OWNERS)(fn)

    def collect(index):
        @owner
        def _():
            drain(boxes[index].at[pl.ds(1, 15)], rs_recv.at[index])
            circles[index][cy] = shares[index](red, me)[...] + jnp.sum(boxes[index][1:16], axis=0)
            for device in rings["y"]:
                here = circles[index].at[cy]
                pltpu.make_async_remote_copy(
                    src_ref=here, dst_ref=here, send_sem=ring_send.at[index], recv_sem=ring_recv.at[index],
                    device_id=device, device_id_type=MESH,
                ).start()

    def hand_out(index, j, device, d):
        share = shares[index](full, j)
        return pltpu.make_async_remote_copy(
            src_ref=share, dst_ref=share, send_sem=ag_send.at[index], recv_sem=ag_recv.at[index, d],
            device_id=device, device_id_type=MESH,
        )

    def pass_on(index, j):
        share = shares[index](full, j)
        core_copy(min(2 + index, 3), share, share).start()

    def finish(index):
        @owner
        def _():
            drain(circles[index].at[pl.ds(0, 3)], ring_recv.at[index])
            terms = [circles[index][y] for y in range(4)]
            shares[index](full, me)[...] = ((terms[0] + terms[1]) + (terms[2] + terms[3])) * scale
            for dx, dz in plane:
                hand_out(index, me, chip(*step(dx, 0, dz)), dx * 4 + dz).start()
            pass_on(index, me)

    def gather(index):
        for dx, dz in reversed(plane):
            x, y, z = step(4 - dx, 0, 4 - dz)
            j = x * 4 + z

            @pl.when(j < OWNERS)
            def _(device=chip(x, y, z), j=j, d=dx * 4 + dz):
                hand_out(index, j, device, d).wait_recv()
                pass_on(index, j)

    pl.semaphore_wait(plane_sem, 3)
    pairs[0].wait_recv()
    mid = mid_part(red, core)
    mid[...] = mid[...] + core_box[BLOCK : BLOCK + STREAM]
    exchange(0)
    pairs[1].wait_recv()
    late = late_part(red, core)
    late[...] = late[...] + core_box[0:BLOCK]
    recv_halos(0, (FAR,))
    send_halos(1, (FAR,))
    put(far_a, weight_terms((far_x,), far_a, range(NY)), True)
    exchange(1)
    exchange(2)
    exchange(3)
    collect(0)
    loads[2].wait()
    for c in range(3):
        lf[c * C : (c + 1) * C, :] = jnp.concatenate([w[ab * 3 + c] for ab in range(9)], axis=1)
        lb[c * C : (c + 1) * C, :] = jnp.concatenate(
            [w[26 - (ab * 3 + c)].T for ab in range(9)], axis=1
        )
    conv(near_x, pf, lf, out)
    conv(far_x, pf, lf, out)
    recv_halos(1, (SAME, NEAR))
    corners(1, lambda copy: copy.start())
    collect(1)
    collect(2)
    collect(3)
    finish(0)
    corners(1, lambda copy: copy.wait_recv())
    conv(near_x, pc, lb, grad_in)
    finish(1)
    finish(2)
    finish(3)
    gather(0)
    recv_halos(1, (FAR,))
    conv(far_x, pc, lb, grad_in)
    gather(1)
    gather(2)
    gather(3)
    for which in range(2):
        done_halos(which, (NEAR, SAME, FAR))
        corners(which, lambda copy: copy.wait_send())
    for copy in pairs:
        copy.wait_send()
    for index, slots in enumerate(boxes):
        owner(lambda: drain(slots.at[pl.ds(0, OWNERS - 1)], rs_send.at[index]))
        pl.when(me >= OWNERS)(lambda: drain(slots.at[pl.ds(0, OWNERS)], rs_send.at[index]))
        owner(lambda: drain(circles[index].at[pl.ds(0, 3)], ring_send.at[index]))
        owner(lambda: drain(slots.at[pl.ds(0, 15)], ag_send.at[index]))
    for index, part in enumerate((mid_part, late_part)):
        passed = part(full, other)
        core_copy(2 + index, passed, passed).wait()


def hand_on(a, b, c, x, y, z, unpacked, sem):
    copies = [
        pltpu.make_async_copy(a, x, sem.at[3]),
        pltpu.make_async_copy(b, y, sem.at[4]),
    ]
    for copy in copies:
        copy.start()
    for k in range(3):
        tiles = c[BLOCK * k : BLOCK * k + 81]
        left = tiles[0:36].reshape(3 * C, 128)
        right = tiles[36:72].reshape(3 * C, 128)
        rest = tiles[72:81].reshape(72, 128)
        rest = jnp.concatenate([rest[:, 32 * q : 32 * q + 32] for q in range(4)], axis=0)
        blocks = (
            left[:, 0:C],
            jnp.concatenate([left[:, C:128], right[:, 0:64]], axis=1),
            jnp.concatenate([right[:, 64:128], rest], axis=1),
        )
        for i, block in enumerate(blocks):
            unpacked[9 * k + 3 * i : 9 * k + 3 * i + 3] = block.reshape(3, C, C)
        part = pl.ds(9 * k, 9)
        copies.append(pltpu.make_async_copy(unpacked.at[part], z.at[part], sem.at[k]))
        copies[-1].start()
    for copy in copies:
        copy.wait()


def shards(features, cotangent, weights, ground, thick):
    voxels = NX * NY * NZ * lax.axis_size("gx") * lax.axis_size("gy")
    block = jax.ShapeDtypeStruct((C, NX, NY, NZ), BF16)
    hbm = pl.BlockSpec(memory_space=pltpu.HBM)
    vmem = pl.BlockSpec(memory_space=pltpu.VMEM)

    def body(*refs):
        kernel(1.0 / math.sqrt(voxels), *refs)

    dma = pltpu.SemaphoreType.DMA
    inner = pltpu.VMEM((C, NX, NY, NZ), BF16)
    results = pl.pallas_call(
        body,
        out_shape=(inner, inner, pltpu.VMEM((3 * BLOCK, 8, 128), F32)),
        in_specs=[hbm] * 5,
        out_specs=(vmem, vmem, vmem),
        scratch_shapes=[
            inner,
            inner,
            pltpu.VMEM((27, C, C), BF16),
            pltpu.SMEM((NX, NY), jnp.int32),
            pltpu.SMEM((NX, NY), jnp.int32),
            pltpu.VMEM((NX + 2, NY + 2, C, NZ), BF16),
            pltpu.VMEM((NX + 2, NY + 2, C, NZ), BF16),
            pltpu.VMEM((C * NY, NZ), F32),
            pltpu.VMEM((NX, 3 * C, NY * NZ), BF16),
            pltpu.VMEM((3 * C, 9 * C), BF16),
            pltpu.VMEM((3 * C, 9 * C), BF16),
            pltpu.VMEM((3 * BLOCK, 8, 128), F32),
            pltpu.VMEM((BLOCK + STREAM, 8, 128), F32),
            pltpu.VMEM((16, 3, 8, 128), F32),
            pltpu.VMEM((3, 16, 2, 8, 128), F32),
            pltpu.VMEM((4, 3, 8, 128), F32),
            pltpu.VMEM((3, 4, 2, 8, 128), F32),
            pltpu.VMEM((C * NY, NZ), F32),
            dma((5,)),
            dma((2, 3, 3)),
            dma((2, 3, 3)),
            dma((4,)),
            dma((4,)),
            dma((4,)),
            dma((4,)),
            dma((4,)),
            dma((4, 16)),
            dma((4,)),
            dma((4,)),
            pltpu.SemaphoreType.REGULAR,
        ],
        compiler_params=pltpu.CompilerParams(
            collective_id=0, has_side_effects=True, vmem_limit_bytes=48 * 1024 * 1024
        ),
        cost_estimate=pl.CostEstimate(
            flops=3 * 2 * NX * NY * NZ * 27 * C * C, bytes_accessed=4 * 2**20, transcendentals=0
        ),
    )(*[pltpu.with_memory_space_constraint(v, pltpu.HBM) for v in (features, cotangent, weights, ground, thick)])
    return pl.pallas_call(
        hand_on,
        out_shape=(block, block, jax.ShapeDtypeStruct((27, C, C), F32)),
        in_specs=[vmem] * 3,
        out_specs=(hbm,) * 3,
        scratch_shapes=[pltpu.VMEM((27, C, C), F32), dma((5,))],
        compiler_params=pltpu.CompilerParams(vmem_limit_bytes=16 * 1024 * 1024),
    )(*results)


def solution(mesh):
    assert mesh.shape["gx"] == 16 and mesh.shape["gy"] == 8
    placed = (
        P(None, "gx", "gy", None),
        P(None, "gx", "gy", None),
        P(),
        P("gx", "gy"),
        P("gx", "gy"),
    )
    return jax.shard_map(
        shards,
        mesh=mesh,
        in_specs=placed,
        out_specs=(P(None, "gx", "gy", None), P(None, "gx", "gy", None), P()),
        check_vma=False,
    )
```

```python
import math

import jax
import jax.numpy as jnp
from jax import lax
from jax.experimental import pallas as pl
from jax.experimental.pallas import tpu as pltpu
from jax.sharding import PartitionSpec as P

MESH = pl.DeviceIdType.MESH
F32 = jnp.float32
BF16 = jnp.bfloat16
C = 96
NX, NY, NZ = 2, 8, 128
OWNERS = 14
BLOCK = 84
STREAM = 42
NEAR, FAR, SAME = 0, 1, 2
NT = (((1,), (1,)), ((), ()))


def kernel(
    scale,
    feat_hbm, cot_hbm, w_hbm, ground_hbm, thick_hbm,
    out, grad_in, full,
    feat, cot, w, ground, thick, pf, pc, tmp, shifted, lf, lb, red, core_box, mid_box, late_box, mid_ring, late_ring, tout,
    load_sem, halo_send, halo_recv, core_send, core_recv,
    rs_send, rs_recv, ag_send, ag_recv, ring_send, ring_recv, plane_sem,
):
    gx = lax.axis_index("gx")
    gy = lax.axis_index("gy")
    core = lax.rem(gx, 2)
    cx = lax.div(gx, 4)
    cy = lax.rem(lax.div(gx, 2), 2) * 2 + lax.rem(gy, 2)
    cz = lax.div(gy, 2)
    near_gx = gx + 1 - 2 * core
    far_gx = gx - 1 + 2 * core
    has_far = jnp.logical_and(far_gx >= 0, far_gx < 16)
    near_x = 1 - core
    far_x = core
    near_a = 2 * (1 - core)
    far_a = 2 * core

    loads = [
        pltpu.make_async_copy(feat_hbm, feat, load_sem.at[0]),
        pltpu.make_async_copy(cot_hbm, cot, load_sem.at[1]),
        pltpu.make_async_copy(w_hbm, w, load_sem.at[2]),
        pltpu.make_async_copy(ground_hbm, ground, load_sem.at[3]),
        pltpu.make_async_copy(thick_hbm, thick, load_sem.at[4]),
    ]
    for load in loads:
        load.start()

    def chip(x, y, z):
        return (x * 4 + lax.div(y, 2) * 2 + core, z * 2 + lax.rem(y, 2))

    def step(dx, dy, dz):
        return lax.rem(cx + dx, 4), lax.rem(cy + dy, 4), lax.rem(cz + dz, 4)

    has_dy = {-1: gy > 0, 0: None, 1: gy < 7}

    def present(side, dy):
        terms = []
        if side == FAR:
            terms.append(has_far)
        if dy != 0:
            terms.append(has_dy[dy])
        if not terms:
            return None
        return terms[0] if len(terms) == 1 else jnp.logical_and(*terms)

    def when(cond, fn):
        if cond is None:
            fn()
        else:
            pl.when(cond)(fn)

    def halo_device(side, dy):
        return ({NEAR: near_gx, FAR: far_gx, SAME: gx}[side], gy + dy)

    halos = [(SAME, -1), (SAME, 1), (FAR, 0), (FAR, -1), (FAR, 1), (NEAR, 0)]
    rings = {
        "x": [chip(*step(d, 0, 0)) for d in (1, 2, 3)],
        "y": [chip(*step(0, d, 0)) for d in (1, 2, 3)],
        "z": [chip(*step(0, 0, d)) for d in (1, 2, 3)],
    }

    def signal(sem, device):
        pl.semaphore_signal(sem, inc=1, device_id=device, device_id_type=MESH)

    barrier = pltpu.get_barrier_semaphore()
    for side, dy in halos:
        when(present(side, dy), lambda side=side, dy=dy: signal(barrier, halo_device(side, dy)))
    for axis in "xyz":
        for device in rings[axis]:
            signal(barrier, device)

    rows = lax.broadcasted_iota(jnp.int32, (NY, NZ), 0)
    heights = lax.broadcasted_iota(jnp.int32, (NY, NZ), 1)

    def occupied(x):
        low = jnp.zeros((NY, NZ), jnp.int32)
        high = jnp.zeros((NY, NZ), jnp.int32)
        for y in range(NY):
            g = ground[x, y]
            low = jnp.where(rows == y, g, low)
            high = jnp.where(rows == y, g + thick[x, y], high)
        return jnp.logical_and(heights >= low, heights < high)

    def columns(src, dst, x, shifts):
        value = jnp.where(occupied(x)[None], src[:, x].astype(F32), 0.0)
        tmp[...] = value.reshape(C * NY, NZ)
        for y in range(NY):
            col = tmp[pl.ds(y, C, stride=NY), :]
            dst[x + 1, y + 1] = col.astype(BF16)
            if shifts:
                lanes = slice(y * NZ, (y + 1) * NZ)
                shifted[x, 0:C, lanes] = pltpu.roll(col, NZ - 1, 1).astype(BF16)
                shifted[x, C : 2 * C, lanes] = col.astype(BF16)
                shifted[x, 2 * C : 3 * C, lanes] = pltpu.roll(col, 1, 1).astype(BF16)

    loads[3].wait()
    loads[4].wait()
    loads[0].wait()
    for x in range(NX):
        columns(feat, pf, x, False)

    n_dy = jnp.where(gy > 0, 1, 0) + jnp.where(gy < 7, 1, 0)
    n_far = jnp.where(has_far, 1, 0)
    pl.semaphore_wait(barrier, n_dy + n_far * (n_dy + 1) + 1 + 9)

    src_y = {-1: 1, 0: 1, 1: NY}
    dst_y = {-1: NY + 1, 0: 1, 1: 0}
    len_y = {-1: 1, 0: NY, 1: 1}

    def halo_copy(which, side, dy):
        buf = (pf, pc)[which]
        n = len_y[dy]
        if side == SAME:
            src_x = dst_x = pl.ds(1, 2)
        elif side == NEAR:
            src_x, dst_x = pl.ds(2 - core, 1), pl.ds(3 * core, 1)
        else:
            src_x, dst_x = pl.ds(1 + core, 1), pl.ds(3 * (1 - core), 1)
        return pltpu.make_async_remote_copy(
            src_ref=buf.at[src_x, pl.ds(src_y[dy], n)],
            dst_ref=buf.at[dst_x, pl.ds(dst_y[dy], n)],
            send_sem=halo_send.at[which, side, dy + 1],
            recv_sem=halo_recv.at[which, side, dy + 1],
            device_id=halo_device(side, dy),
            device_id_type=MESH,
        )

    def send_halos(which, sides=(SAME, FAR, NEAR)):
        for side, dy in halos:
            if side in sides:
                when(present(side, dy), lambda side=side, dy=dy: halo_copy(which, side, dy).start())

    def recv_halos(which, sides):
        for side, dy in halos:
            if side in sides:
                when(present(side, -dy), lambda side=side, dy=dy: halo_copy(which, side, dy).wait_recv())

    def done_halos(which, sides):
        for side, dy in halos:
            if side in sides:
                when(present(side, dy), lambda side=side, dy=dy: halo_copy(which, side, dy).wait_send())

    def corner_copy(which, e):
        buf = (pf, pc)[which]
        y = pl.ds(0 if e < 0 else NY + 1, 1)
        return pltpu.make_async_remote_copy(
            src_ref=buf.at[pl.ds(2 - core, 1), y],
            dst_ref=buf.at[pl.ds(3 * core, 1), y],
            send_sem=halo_send.at[which, NEAR, e + 1],
            recv_sem=halo_recv.at[which, NEAR, e + 1],
            device_id=(near_gx, gy),
            device_id_type=MESH,
        )

    def corners(which, act):
        for e in (-1, 1):
            pl.when(has_dy[e])(lambda e=e: act(corner_copy(which, e)))

    def clear_edges(buf):
        zeros = jnp.zeros((C, NZ), BF16)

        def far_side():
            for y in range(NY + 2):
                buf[3 * core, y] = zeros

        def y_side(y):
            for x in range(NX + 2):
                buf[x, y] = zeros

        pl.when(jnp.logical_not(has_far))(far_side)
        pl.when(gy == 0)(lambda: y_side(0))
        pl.when(gy == 7)(lambda: y_side(NY + 1))

    send_halos(0)
    for device in rings["z"]:
        signal(plane_sem, device)
    loads[1].wait()
    for x in range(NX):
        columns(cot, pc, x, True)
    send_halos(1, (SAME, NEAR))

    def weight_terms(xs, a, ys, cut=slice(None)):
        lhs = jnp.concatenate([shifted[x, :, y * NZ : (y + 1) * NZ] for x in xs for y in ys], axis=1)
        rhs = jnp.concatenate(
            [jnp.concatenate([pf[x + a, y + b] for x in xs for y in ys], axis=1) for b in range(3)],
            axis=0,
        )
        return lax.dot_general(lhs, rhs[cut], NT, preferred_element_type=F32)

    def put(a, value, add):
        rest = jnp.concatenate([value[72 * q : 72 * q + 72, 256:288] for q in range(4)], axis=1)
        parts = (
            (0, 36, value[:, 0:128]), (36, 36, value[:, 128:256]), (72, 9, rest),
        )
        for start, n, part in parts:
            at = pl.ds(BLOCK * a + start, n)
            part = part.reshape(n, 8, 128)
            red[at] = red[at] + part if add else part
        if not add:
            red[pl.ds(BLOCK * a + 81, 3)] = jnp.zeros((3, 8, 128), F32)

    def core_copy(k, src, dst):
        return pltpu.make_async_remote_copy(
            src_ref=src, dst_ref=dst, send_sem=core_send.at[k], recv_sem=core_recv.at[k],
            device_id=(near_gx, gy), device_id_type=MESH,
        )

    def late_part(buf, m):
        return buf.at[pl.ds(2 * BLOCK * m, BLOCK)]

    def mid_part(buf, m):
        return buf.at[pl.ds(BLOCK + STREAM * m, STREAM)]

    other = 1 - core
    inner, outer, both = range(1, NY - 1), (0, NY - 1), (near_x, far_x)
    put(1, weight_terms(both, 1, inner), False)
    put(far_a, weight_terms((near_x,), far_a, inner), False)
    clear_edges(pf)
    clear_edges(pc)
    recv_halos(0, (NEAR,))
    put(near_a, weight_terms(both, near_a, inner), False)
    recv_halos(0, (SAME,))
    corners(0, lambda copy: copy.start())
    put(1, weight_terms(both, 1, outer), True)
    pairs = [core_copy(0, mid_part(red, other), core_box.at[pl.ds(BLOCK, STREAM)])]
    pairs[0].start()
    put(far_a, weight_terms((near_x,), far_a, outer), True)
    corners(0, lambda copy: copy.wait_recv())
    put(near_a, weight_terms(both, near_a, outer), True)
    pairs.append(core_copy(1, late_part(red, other), core_box.at[pl.ds(0, BLOCK)]))
    pairs[1].start()

    def conv_pair(x, j, buf, lhs):
        stack = jnp.concatenate(
            [
                jnp.concatenate([buf[x + a, 2 * j + b], buf[x + a, 2 * j + b + 1]], axis=1)
                for a in range(3)
                for b in range(3)
            ],
            axis=0,
        )
        prod = jnp.dot(lhs[...], stack, preferred_element_type=F32)
        for half in range(2):
            part = prod[:, half * NZ : (half + 1) * NZ]
            col = (
                pltpu.roll(part[0:C], 1, 1) + part[C : 2 * C] + pltpu.roll(part[2 * C : 3 * C], NZ - 1, 1)
            )
            tout[pl.ds(2 * j + half, C, stride=NY), :] = col

    def conv(x, buf, lhs, dst):
        for j in range(NY // 2):
            conv_pair(x, j, buf, lhs)
        mask = occupied(x)
        dst[:, x] = jnp.where(mask[None], tout[...].reshape(C, NY, NZ), 0.0).astype(BF16)

    me = cx * 4 + cz
    plane = sorted(
        [(dx, dz) for dx in range(4) for dz in range(4) if (dx, dz) != (0, 0)],
        key=lambda d: -sum(min(v, 4 - v) for v in d),
    )

    def stream(base, n):
        return lambda buf, j: buf.at[pl.ds(base + n * j, n)]

    shares = [stream(BLOCK + STREAM * core, 3)]
    shares += [stream(2 * BLOCK * core + 2 * OWNERS * i, 2) for i in range(3)]
    boxes = [mid_box] + [late_box.at[i] for i in range(3)]
    circles = [mid_ring] + [late_ring.at[i] for i in range(3)]

    def exchange(index):
        for dx, dz in plane:
            x, y, z = step(dx, 0, dz)
            j = x * 4 + z

            @pl.when(j < OWNERS)
            def _(device=chip(x, y, z), j=j, d=dx * 4 + dz):
                pltpu.make_async_remote_copy(
                    src_ref=shares[index](red, j), dst_ref=boxes[index].at[d],
                    send_sem=rs_send.at[index], recv_sem=rs_recv.at[index],
                    device_id=device, device_id_type=MESH,
                ).start()

    def drain(ref, sem):
        pltpu.make_async_copy(ref, ref, sem).wait()

    def owner(fn):
        pl.when(me < OWNERS)(fn)

    def collect(index):
        @owner
        def _():
            drain(boxes[index].at[pl.ds(1, 15)], rs_recv.at[index])
            circles[index][cy] = shares[index](red, me)[...] + jnp.sum(boxes[index][1:16], axis=0)
            for device in rings["y"]:
                here = circles[index].at[cy]
                pltpu.make_async_remote_copy(
                    src_ref=here, dst_ref=here, send_sem=ring_send.at[index], recv_sem=ring_recv.at[index],
                    device_id=device, device_id_type=MESH,
                ).start()

    def hand_out(index, j, device, d):
        share = shares[index](full, j)
        return pltpu.make_async_remote_copy(
            src_ref=share, dst_ref=share, send_sem=ag_send.at[index], recv_sem=ag_recv.at[index, d],
            device_id=device, device_id_type=MESH,
        )

    def pass_on(index, j):
        share = shares[index](full, j)
        core_copy(min(2 + index, 3), share, share).start()

    def finish(index):
        @owner
        def _():
            drain(circles[index].at[pl.ds(0, 3)], ring_recv.at[index])
            terms = [circles[index][y] for y in range(4)]
            shares[index](full, me)[...] = ((terms[0] + terms[1]) + (terms[2] + terms[3])) * scale
            for dx, dz in plane:
                hand_out(index, me, chip(*step(dx, 0, dz)), dx * 4 + dz).start()
            pass_on(index, me)

    def gather(index):
        for dx, dz in reversed(plane):
            x, y, z = step(4 - dx, 0, 4 - dz)
            j = x * 4 + z

            @pl.when(j < OWNERS)
            def _(device=chip(x, y, z), j=j, d=dx * 4 + dz):
                hand_out(index, j, device, d).wait_recv()
                pass_on(index, j)

    pl.semaphore_wait(plane_sem, 3)
    pairs[0].wait_recv()
    mid = mid_part(red, core)
    mid[...] = mid[...] + core_box[BLOCK : BLOCK + STREAM]
    exchange(0)
    pairs[1].wait_recv()
    late = late_part(red, core)
    late[...] = late[...] + core_box[0:BLOCK]
    recv_halos(0, (FAR,))
    send_halos(1, (FAR,))
    head = weight_terms((far_x,), far_a, range(NY), slice(0, 128))
    at = pl.ds(BLOCK * far_a, 36)
    red[at] = red[at] + head.reshape(36, 8, 128)
    exchange(1)
    tail = weight_terms((far_x,), far_a, range(NY), slice(128, 288))
    rest = jnp.concatenate([tail[72 * q : 72 * q + 72, 128:160] for q in range(4)], axis=1)
    at = pl.ds(BLOCK * far_a + 36, 36)
    red[at] = red[at] + tail[:, 0:128].reshape(36, 8, 128)
    at = pl.ds(BLOCK * far_a + 72, 9)
    red[at] = red[at] + rest.reshape(9, 8, 128)
    exchange(2)
    exchange(3)
    collect(0)
    loads[2].wait()
    for c in range(3):
        lf[c * C : (c + 1) * C, :] = jnp.concatenate([w[ab * 3 + c] for ab in range(9)], axis=1)
        lb[c * C : (c + 1) * C, :] = jnp.concatenate(
            [w[26 - (ab * 3 + c)].T for ab in range(9)], axis=1
        )
    conv(near_x, pf, lf, out)
    conv(far_x, pf, lf, out)
    recv_halos(1, (SAME, NEAR))
    corners(1, lambda copy: copy.start())
    collect(1)
    collect(2)
    collect(3)
    finish(0)
    corners(1, lambda copy: copy.wait_recv())
    conv(near_x, pc, lb, grad_in)
    finish(1)
    finish(2)
    finish(3)
    gather(0)
    recv_halos(1, (FAR,))
    conv(far_x, pc, lb, grad_in)
    gather(1)
    gather(2)
    gather(3)
    for which in range(2):
        done_halos(which, (NEAR, SAME, FAR))
        corners(which, lambda copy: copy.wait_send())
    for copy in pairs:
        copy.wait_send()
    for index, slots in enumerate(boxes):
        owner(lambda: drain(slots.at[pl.ds(0, OWNERS - 1)], rs_send.at[index]))
        pl.when(me >= OWNERS)(lambda: drain(slots.at[pl.ds(0, OWNERS)], rs_send.at[index]))
        owner(lambda: drain(circles[index].at[pl.ds(0, 3)], ring_send.at[index]))
        owner(lambda: drain(slots.at[pl.ds(0, 15)], ag_send.at[index]))
    for index, part in enumerate((mid_part, late_part)):
        passed = part(full, other)
        core_copy(2 + index, passed, passed).wait()


def hand_on(a, b, c, x, y, z, unpacked, sem):
    copies = [
        pltpu.make_async_copy(a, x, sem.at[3]),
        pltpu.make_async_copy(b, y, sem.at[4]),
    ]
    for copy in copies:
        copy.start()
    for k in range(3):
        tiles = c[BLOCK * k : BLOCK * k + 81]
        left = tiles[0:36].reshape(3 * C, 128)
        right = tiles[36:72].reshape(3 * C, 128)
        rest = tiles[72:81].reshape(72, 128)
        rest = jnp.concatenate([rest[:, 32 * q : 32 * q + 32] for q in range(4)], axis=0)
        blocks = (
            left[:, 0:C],
            jnp.concatenate([left[:, C:128], right[:, 0:64]], axis=1),
            jnp.concatenate([right[:, 64:128], rest], axis=1),
        )
        for i, block in enumerate(blocks):
            unpacked[9 * k + 3 * i : 9 * k + 3 * i + 3] = block.reshape(3, C, C)
        part = pl.ds(9 * k, 9)
        copies.append(pltpu.make_async_copy(unpacked.at[part], z.at[part], sem.at[k]))
        copies[-1].start()
    for copy in copies:
        copy.wait()


def shards(features, cotangent, weights, ground, thick):
    voxels = NX * NY * NZ * lax.axis_size("gx") * lax.axis_size("gy")
    block = jax.ShapeDtypeStruct((C, NX, NY, NZ), BF16)
    hbm = pl.BlockSpec(memory_space=pltpu.HBM)
    vmem = pl.BlockSpec(memory_space=pltpu.VMEM)

    def body(*refs):
        kernel(1.0 / math.sqrt(voxels), *refs)

    dma = pltpu.SemaphoreType.DMA
    inner = pltpu.VMEM((C, NX, NY, NZ), BF16)
    results = pl.pallas_call(
        body,
        out_shape=(inner, inner, pltpu.VMEM((3 * BLOCK, 8, 128), F32)),
        in_specs=[hbm] * 5,
        out_specs=(vmem, vmem, vmem),
        scratch_shapes=[
            inner,
            inner,
            pltpu.VMEM((27, C, C), BF16),
            pltpu.SMEM((NX, NY), jnp.int32),
            pltpu.SMEM((NX, NY), jnp.int32),
            pltpu.VMEM((NX + 2, NY + 2, C, NZ), BF16),
            pltpu.VMEM((NX + 2, NY + 2, C, NZ), BF16),
            pltpu.VMEM((C * NY, NZ), F32),
            pltpu.VMEM((NX, 3 * C, NY * NZ), BF16),
            pltpu.VMEM((3 * C, 9 * C), BF16),
            pltpu.VMEM((3 * C, 9 * C), BF16),
            pltpu.VMEM((3 * BLOCK, 8, 128), F32),
            pltpu.VMEM((BLOCK + STREAM, 8, 128), F32),
            pltpu.VMEM((16, 3, 8, 128), F32),
            pltpu.VMEM((3, 16, 2, 8, 128), F32),
            pltpu.VMEM((4, 3, 8, 128), F32),
            pltpu.VMEM((3, 4, 2, 8, 128), F32),
            pltpu.VMEM((C * NY, NZ), F32),
            dma((5,)),
            dma((2, 3, 3)),
            dma((2, 3, 3)),
            dma((4,)),
            dma((4,)),
            dma((4,)),
            dma((4,)),
            dma((4,)),
            dma((4, 16)),
            dma((4,)),
            dma((4,)),
            pltpu.SemaphoreType.REGULAR,
        ],
        compiler_params=pltpu.CompilerParams(
            collective_id=0, has_side_effects=True, vmem_limit_bytes=48 * 1024 * 1024
        ),
        cost_estimate=pl.CostEstimate(
            flops=3 * 2 * NX * NY * NZ * 27 * C * C, bytes_accessed=4 * 2**20, transcendentals=0
        ),
    )(*[pltpu.with_memory_space_constraint(v, pltpu.HBM) for v in (features, cotangent, weights, ground, thick)])
    return pl.pallas_call(
        hand_on,
        out_shape=(block, block, jax.ShapeDtypeStruct((27, C, C), F32)),
        in_specs=[vmem] * 3,
        out_specs=(hbm,) * 3,
        scratch_shapes=[pltpu.VMEM((27, C, C), F32), dma((5,))],
        compiler_params=pltpu.CompilerParams(vmem_limit_bytes=16 * 1024 * 1024),
    )(*results)


def solution(mesh):
    assert mesh.shape["gx"] == 16 and mesh.shape["gy"] == 8
    placed = (
        P(None, "gx", "gy", None),
        P(None, "gx", "gy", None),
        P(),
        P("gx", "gy"),
        P("gx", "gy"),
    )
    return jax.shard_map(
        shards,
        mesh=mesh,
        in_specs=placed,
        out_specs=(P(None, "gx", "gy", None), P(None, "gx", "gy", None), P()),
        check_vma=False,
    )
```
